32 devices in a mesh: groups: 2 (over y), ctx: 4 (over z), chan: 4 (over x, core).
Axes of the slice: x: 2, y: 2, z: 4, core: 2. Of those that a mesh axis runs over, the one named last changes fastest.
Arguments:
- projected: bfloat16 [3, 2048, 4096], P(None, ('groups', 'ctx'), 'chan'), parts along dimension 1, may hold values from -6 to 6
- short_filter: float32 [3, 3, 4096], P(None, None, 'chan'), may hold values from -3 to 3
- decay_rates: float32 [16, 4096], P(None, 'chan'), may hold values from 0.0001953125 to 0.05
- residues: float32 [16, 4096], P(None, 'chan'), may hold values from -1.5 to 1.5
- skip_gain: float32 [4096], P('chan'), may hold values from -4 to 4
- out_weight: bfloat16 [4096, 2048], P('chan'), may hold values from -0.09375 to 0.09375
Outputs:
- layer_out: bfloat16 [2048, 2048], P(('groups', 'ctx'), 'chan'), parts along dimension 0
The draws below stay inside these ranges and needn't reach their ends.
There are 2 independent parts, one for each index of `groups`. The reference program is written for one: setup_inputs(seed, part) draws one part's arguments, and reference() takes and returns one part's arrays. A program takes and returns all parts, laid end to end along the dimension named above; an argument that names none is the same for every part. Nothing has to cross between parts.
All inputs are finite; a program needn't handle non-finite values.
Results may differ from the reference program's by a relative error of at most 0.012.
Values may be sent and summed in bfloat16 or wider, within the bound.
A program may use at most 128 MiB of HBM per device.

```python
import math
import jax
import jax.numpy as jnp

WIDTH = 4096
OUTW = 2048
MODES = 16
SEQ = 1024


def level_of(key, dims, pieces, low, high):
    factor_of, own = 1.0, jax.random.fold_in(key, 6)
    for dim, shards_of in pieces:
        steps = jnp.exp(jax.random.uniform(jax.random.fold_in(own, dim), (shards_of,), jnp.float32, low / len(pieces), high / len(pieces)))
        factor_of = factor_of * jnp.repeat(steps, dims[dim] // shards_of).reshape([-1 if axis == dim else 1 for axis in range(len(dims))])
    return factor_of


def gaussian(key, shape, width, bound, shards=(), kind=jnp.bfloat16):
    gain = level_of(key, shape, shards, -0.22, 0.18) if shards else 1.0
    entries = jax.random.normal(key, shape, jnp.float32) * width * gain
    return jnp.minimum(jnp.maximum(entries, -bound), bound).astype(kind)


def setup_inputs(seed: int = 0, part: int = 0) -> dict:
    key_of = jax.random.split(jax.random.key(seed), 7)
    part_splits = jax.random.split(jax.random.fold_in(key_of[6], part), 7)
    projected = gaussian(part_splits[0], (3, SEQ, WIDTH), 1.0, 6.0, ((1, 4), (2, 4)))
    short_filter = gaussian(key_of[1], (3, 3, WIDTH), 0.6, 3.0, ((2, 4),), jnp.float32)
    decay_rates = jnp.clip(jnp.exp(math.log(0.05) - 5.5451774 * jax.random.uniform(key_of[2], (MODES, WIDTH), jnp.float32) ** level_of(key_of[2], (MODES, WIDTH), ((1, 4),), -0.2, 0.2)), 0.0001953125, 0.05)
    residues = gaussian(key_of[3], (MODES, WIDTH), 0.25, 1.5, ((1, 4),), jnp.float32)
    skip_gain = gaussian(key_of[4], (WIDTH,), 1.0, 4.0, ((0, 4),), jnp.float32)
    out_weight = gaussian(key_of[5], (WIDTH, OUTW), WIDTH ** -0.5, 0.09375, ((0, 4),))
    return {"projected": projected, "short_filter": short_filter, "decay_rates": decay_rates, "residues": residues, "skip_gain": skip_gain, "out_weight": out_weight}


def reference(projected, short_filter, decay_rates, residues, skip_gain, out_weight):
    values = projected.astype(jnp.float32)
    padded = jnp.pad(values, ((0, 0), (2, 0), (0, 0)))
    mixed = short_filter[:, 0, None, :] * padded[:, 2:, :]
    mixed = mixed + short_filter[:, 1, None, :] * padded[:, 1:-1, :]
    mixed = mixed + short_filter[:, 2, None, :] * padded[:, :-2, :]
    query = mixed[0]
    gated = (mixed[1] * mixed[2]).astype(jnp.bfloat16)
    gated_f = gated.astype(jnp.float32)
    scaled = residues * jnp.sqrt(-jnp.expm1(-2.0 * decay_rates))
    times = jnp.arange(SEQ, dtype=jnp.float32)
    filt = jnp.zeros((SEQ, WIDTH), jnp.float32)
    for mode in range(MODES):
        filt = filt + scaled[mode][None, :] * jnp.exp(-decay_rates[mode][None, :] * times[:, None])
    spectrum = jnp.fft.rfft(gated_f, n=2 * SEQ, axis=0) * jnp.fft.rfft(filt, n=2 * SEQ, axis=0)
    conv = jnp.fft.irfft(spectrum, n=2 * SEQ, axis=0)[:SEQ].astype(jnp.float32)
    mixed_out = (query * (conv + skip_gain[None, :] * gated_f)).astype(jnp.bfloat16)
    return jnp.dot(mixed_out, out_weight, preferred_element_type=jnp.float32).astype(jnp.bfloat16)
```

```python
import functools

import jax
import jax.numpy as jnp
from jax import lax
from jax.experimental import pallas as pl
from jax.experimental.pallas import tpu as pltpu
from jax.sharding import PartitionSpec as P

MESH = pl.DeviceIdType.MESH
LANES = 128
SUB = 8
STEP = 16
CHUNKS = 2


def expm1(v):
    series = jnp.ones_like(v)
    for order in range(9, 1, -1):
        series = 1.0 + series * v * (1.0 / order)
    return jnp.where(v > -0.3, v * series, jnp.exp(v) - 1.0)


def rows(token, count=1):
    start = token * SUB
    if not isinstance(start, int):
        start = pl.multiple_of(start, SUB)
    return pl.ds(start, count * SUB)


def kernel(
    n, m, proj_hbm, sf_ref, dr_ref, re_ref, sg_ref, w_hbm, out_ref,
    proj, wv, sft, dec, res, skip, decay, gain, passing, first_pow,
    x, q, g, y, mo, own, arrived, carried, ss, sr, xs, xr, acc,
    proj_sem, w_sem, edge_sem, state_send, state_recv, sib_send, sib_recv, far_send, far_recv,
):
    length, width = proj.shape[1:]
    modes = dr_ref.shape[0]
    blocks = width // LANES
    half = m // 2
    out_w = out_ref.shape[1]
    part = length // CHUNKS
    z, c = lax.axis_index("ctx"), lax.axis_index("chan")
    hi, lo = c // 2, lax.rem(c, 2)
    sibling = hi * 2 + (1 - lo)

    def far(o):
        return lax.rem(hi + o, half) * 2 + lo

    barrier = pltpu.get_barrier_semaphore()
    for off in range(1, n):
        pl.semaphore_signal(barrier, inc=1, device_id={"ctx": lax.rem(z + off, n)}, device_id_type=MESH)
    pl.semaphore_signal(barrier, inc=1, device_id={"chan": sibling}, device_id_type=MESH)
    for o in range(1, half):
        pl.semaphore_signal(barrier, inc=1, device_id={"chan": far(o)}, device_id_type=MESH)

    proj_copy = pltpu.make_async_copy(proj_hbm, proj, proj_sem)
    proj_copy.start()

    def w_copy(o, who):
        target = lax.rem(hi + o, half) * 2 + (lo if who else 1 - lo)
        columns = pl.ds(pl.multiple_of(target * out_w, LANES), out_w)
        slot = 2 * o + who
        return pltpu.make_async_copy(w_hbm.at[:, columns], wv.at[slot], w_sem.at[slot])

    for o in range(half):
        for who in range(2):
            w_copy(o, who).start()

    if blocks < SUB:
        for buffer in (sft, dec, res, skip, x):
            buffer[...] = jnp.zeros_like(buffer)
    for j in range(blocks):
        lanes = pl.ds(j * LANES, LANES)
        dec[pl.ds(j, modes, stride=SUB), :] = dr_ref[:, lanes]
        res[pl.ds(j, modes, stride=SUB), :] = re_ref[:, lanes]
        skip[pl.ds(j, 1), :] = sg_ref[:, lanes]
        for comp in range(3):
            sft[pl.ds(comp * 3 * SUB + j, 3, stride=SUB), :] = sf_ref[comp, :, lanes]
    rate = dec[...]
    decay[...] = jnp.exp(-rate)
    gain[...] = res[...] * jnp.sqrt(-expm1(-2.0 * rate))
    passing[...] = jnp.exp(-rate * float(length))
    first_pow[...] = jnp.exp(-rate * float(length - 2))

    proj_copy.wait()

    @pl.loop(0, length // STEP)
    def _(i):
        t = pl.multiple_of(i * STEP, STEP)
        for comp in range(3):
            for j in range(blocks):
                piece = proj[comp, pl.ds(t, STEP), pl.ds(j * LANES, LANES)].astype(jnp.float32)
                x[comp, pl.ds((t + 2) * SUB + j, STEP, stride=SUB), :] = piece

    pl.semaphore_wait(barrier, (n - 1) + 1 + (half - 1))

    edge = pltpu.make_async_remote_copy(
        src_ref=x.at[:, pl.ds(length * SUB, 2 * SUB), :],
        dst_ref=x.at[:, pl.ds(0, 2 * SUB), :],
        send_sem=edge_sem.at[0],
        recv_sem=edge_sem.at[1],
        device_id={"ctx": lax.rem(z + 1, n)},
        device_id_type=MESH,
    )

    @pl.when(z < n - 1)
    def _():
        edge.start()

    def mode(ref, k):
        return ref[pl.ds(k * SUB, SUB), :]

    def mix(t, count):
        taps = [sft[pl.ds(k * SUB, SUB), :] for k in range(9)]

        def one(comp):
            total = None
            for lag in range(3):
                value = x[comp, rows(t + 2 - lag, count), :].reshape(count, SUB, LANES)
                value = taps[comp * 3 + lag][None] * value
                total = value if total is None else total + value
            return total

        q[rows(t, count), :] = one(0).reshape(count * SUB, LANES)
        gated = (one(1) * one(2)).astype(jnp.bfloat16).astype(jnp.float32)
        g[rows(t, count), :] = gated.reshape(count * SUB, LANES)
        return gated

    def horner(state, gated, count):
        for s in range(count):
            state = [mode(decay, k) * state[k] + gated[s] for k in range(modes)]
        return state

    state = horner([jnp.zeros((SUB, LANES), jnp.float32)] * modes, mix(2, SUB - 2), SUB - 2)

    def own_lap(i, state):
        return tuple(horner(list(state), mix(i * SUB, SUB), SUB))

    state = list(lax.fori_loop(1, length // SUB, own_lap, tuple(state)))

    @pl.when(z == 0)
    def _():
        x[:, pl.ds(0, 2 * SUB), :] = jnp.zeros((3, 2 * SUB, LANES), jnp.float32)

    @pl.when(z > 0)
    def _():
        edge.wait_recv()

    head = mix(0, 2)
    for k in range(0, modes, 2):
        pair = [
            state[k + e] + mode(first_pow, k + e) * (mode(decay, k + e) * head[0] + head[1]) for e in range(2)
        ]
        own[pl.ds(k * SUB, 2 * SUB), :] = jnp.concatenate(pair, axis=0).astype(jnp.bfloat16)

    def send_state(off):
        return pltpu.make_async_remote_copy(
            src_ref=own,
            dst_ref=arrived.at[off - 1],
            send_sem=state_send.at[off - 1],
            recv_sem=state_recv.at[off - 1],
            device_id={"ctx": lax.rem(z + off, n)},
            device_id_type=MESH,
        )

    for off in range(1, n):

        @pl.when(z + off < n)
        def _(off=off):
            send_state(off).start()

    def near_lap(i, state):
        state = list(state)
        for s in range(SUB):
            token = rows(i * SUB + s)
            gated = g[token, :]
            sums = [None] * 4
            for k in range(modes):
                state[k] = mode(decay, k) * state[k] + gated
                term = mode(gain, k) * state[k]
                sums[k % 4] = term if sums[k % 4] is None else sums[k % 4] + term
            y[token, :] = (sums[0] + sums[1]) + (sums[2] + sums[3])
        return tuple(state)

    lax.fori_loop(
        0, length // SUB, near_lap, tuple(jnp.zeros((SUB, LANES), jnp.float32) for _ in range(modes))
    )

    carried[...] = jnp.zeros_like(carried)
    for off in range(n - 1, 0, -1):

        @pl.when(z >= off)
        def _(off=off):
            send_state(off).wait_recv()
            carried[...] = carried[...] * passing[...] + arrived[off - 1].astype(jnp.float32)

    reach = [mode(carried, k) * mode(gain, k) * mode(decay, k) for k in range(modes)]

    def finish_lap(i, reach):
        reach = list(reach)
        for s in range(SUB):
            token = rows(i * SUB + s)
            total = y[token, :] + skip[...] * g[token, :]
            sums = [total, None, None, None]
            for k in range(modes):
                sums[k % 4] = reach[k] if sums[k % 4] is None else sums[k % 4] + reach[k]
                reach[k] = reach[k] * mode(decay, k)
            y[token, :] = q[token, :] * ((sums[0] + sums[1]) + (sums[2] + sums[3]))
        return tuple(reach)

    def gather_lap(i):
        t = pl.multiple_of(i * STEP, STEP)
        for j in range(blocks):
            piece = y[pl.ds(t * SUB + j, STEP, stride=SUB), :]
            mo[pl.ds(t, STEP), pl.ds(j * LANES, LANES)] = piece.astype(jnp.bfloat16)

    def to_sibling(o, p):
        return pltpu.make_async_remote_copy(
            src_ref=ss.at[o, p],
            dst_ref=sr.at[o, p],
            send_sem=sib_send.at[o, p],
            recv_sem=sib_recv.at[o, p],
            device_id={"chan": sibling},
            device_id_type=MESH,
        )

    def to_far(o, p):
        return pltpu.make_async_remote_copy(
            src_ref=xs.at[o - 1, p],
            dst_ref=xr.at[o - 1, p],
            send_sem=far_send.at[o - 1, p],
            recv_sem=far_recv.at[o - 1, p],
            device_id={"chan": far(o)},
            device_id_type=MESH,
        )

    def product(p, slot):
        return jnp.dot(mo[pl.ds(p * part, part), :], wv[slot], preferred_element_type=jnp.float32)

    order = list(range(1, half)) + [0]
    for p in range(CHUNKS):
        first, last = p * part // SUB, (p + 1) * part // SUB
        reach = list(lax.fori_loop(first, last, finish_lap, tuple(reach)))
        pl.loop(p * part // STEP, (p + 1) * part // STEP)(gather_lap)
        for o in order:
            if p == 0:
                w_copy(o, 0).wait()
            ss[o, p] = product(p, 2 * o).astype(jnp.bfloat16)
            to_sibling(o, p).start()
        for o in order:
            if p == 0:
                w_copy(o, 1).wait()
            mine = product(p, 2 * o + 1)
            if o == 0:
                acc[p] = mine
            else:
                to_sibling(o, p).wait_recv()
                xs[o - 1, p] = (mine + sr[o, p].astype(jnp.float32)).astype(jnp.bfloat16)
                to_far(o, p).start()

    for p in range(CHUNKS):
        to_sibling(0, p).wait_recv()
        total = acc[p] + sr[0, p].astype(jnp.float32)
        for o in range(1, half):
            to_far(o, p).wait_recv()
            total = total + xr[o - 1, p].astype(jnp.float32)
        out_ref[pl.ds(p * part, part), :] = total.astype(out_ref.dtype)

    @pl.when(z < n - 1)
    def _():
        edge.wait_send()

    for off in range(1, n):

        @pl.when(z + off < n)
        def _(off=off):
            send_state(off).wait_send()

    for p in range(CHUNKS):
        for o in range(half):
            to_sibling(o, p).wait_send()
        for o in range(1, half):
            to_far(o, p).wait_send()


def body(projected, short_filter, decay_rates, residues, skip_gain, out_weight):
    n, m = lax.axis_size("ctx"), lax.axis_size("chan")
    length, width = projected.shape[1:]
    modes = decay_rates.shape[0]
    out_w = out_weight.shape[1] // m
    half = m // 2
    part = length // CHUNKS
    f32, bf16 = jnp.float32, jnp.bfloat16
    table = pltpu.VMEM((modes * SUB, LANES), f32)
    tokens = pltpu.VMEM((length * SUB, LANES), f32)
    dma = pltpu.SemaphoreType.DMA
    vmem = pl.BlockSpec(memory_space=pltpu.VMEM)
    hbm = pl.BlockSpec(memory_space=pl.ANY)
    return pl.pallas_call(
        functools.partial(kernel, n, m),
        out_shape=jax.ShapeDtypeStruct((length, out_w), bf16),
        in_specs=[hbm, vmem, vmem, vmem, vmem, hbm],
        out_specs=vmem,
        scratch_shapes=[
            pltpu.VMEM((3, length, width), bf16),
            pltpu.VMEM((m, width, out_w), bf16),
            pltpu.VMEM((9 * SUB, LANES), f32),
            table,
            table,
            pltpu.VMEM((SUB, LANES), f32),
            table,
            table,
            table,
            table,
            pltpu.VMEM((3, (length + 2) * SUB, LANES), f32),
            tokens,
            tokens,
            tokens,
            pltpu.VMEM((length, width), bf16),
            pltpu.VMEM((modes * SUB, LANES), bf16),
            pltpu.VMEM((n - 1, modes * SUB, LANES), bf16),
            table,
            pltpu.VMEM((half, CHUNKS, part, out_w), bf16),
            pltpu.VMEM((half, CHUNKS, part, out_w), bf16),
            pltpu.VMEM((half - 1, CHUNKS, part, out_w), bf16),
            pltpu.VMEM((half - 1, CHUNKS, part, out_w), bf16),
            pltpu.VMEM((CHUNKS, part, out_w), f32),
            dma,
            dma((m,)),
            dma((2,)),
            dma((n - 1,)),
            dma((n - 1,)),
            dma((half, CHUNKS)),
            dma((half, CHUNKS)),
            dma((half - 1, CHUNKS)),
            dma((half - 1, CHUNKS)),
        ],
        compiler_params=pltpu.CompilerParams(
            collective_id=0, has_side_effects=True, vmem_limit_bytes=48 * 1024 * 1024
        ),
        cost_estimate=pl.CostEstimate(
            flops=2 * length * width * out_w * m, bytes_accessed=2 * width * out_w * m, transcendentals=0
        ),
        name="hyena_layer",
    )(projected, short_filter, decay_rates, residues, skip_gain.reshape(1, width), out_weight)


def solution(mesh):
    in_specs = (
        P(None, ("groups", "ctx"), "chan"),
        P(None, None, "chan"),
        P(None, "chan"),
        P(None, "chan"),
        P("chan"),
        P("chan", None),
    )
    out_specs = P(("groups", "ctx"), "chan")
    return jax.shard_map(body, mesh=mesh, in_specs=in_specs, out_specs=out_specs, check_vma=False)
```

```python
import functools

import jax
import jax.numpy as jnp
from jax import lax
from jax.experimental import pallas as pl
from jax.experimental.pallas import tpu as pltpu
from jax.sharding import PartitionSpec as P

MESH = pl.DeviceIdType.MESH
LANES = 128
SUB = 8
STEP = 16


def parts_of(length):
    return [(0, length // 4), (length // 4, length // 4), (length // 2, length // 2)]


def expm1(v):
    series = jnp.ones_like(v)
    for order in range(9, 1, -1):
        series = 1.0 + series * v * (1.0 / order)
    return jnp.where(v > -0.3, v * series, jnp.exp(v) - 1.0)


def rows(token, count=1):
    start = token * SUB
    if not isinstance(start, int):
        start = pl.multiple_of(start, SUB)
    return pl.ds(start, count * SUB)


def kernel(
    n, m, proj_hbm, sf_hbm, dr_hbm, re_hbm, sg_hbm, w_hbm, out_ref,
    proj, sf_ref, dr_ref, re_ref, sg_ref, wv, sft, dec, res, skip, decay, gain, passing, first_pow,
    x, q, g, y, mo, own, arrived, carried, ss, sr, xs, xr, acc,
    proj_sem, small_sem, w_sem, edge_send, edge_recv, state_send, state_recv,
    sib_send, sib_recv, far_send, far_recv,
):
    length, width = proj.shape[1:]
    modes = dr_ref.shape[0]
    blocks = width // LANES
    half = m // 2
    out_w = out_ref.shape[1]
    parts = parts_of(length)
    z, c = lax.axis_index("ctx"), lax.axis_index("chan")
    hi, lo = c // 2, lax.rem(c, 2)
    sibling = hi * 2 + (1 - lo)

    def far(o):
        return lax.rem(hi + o, half) * 2 + lo

    barrier = pltpu.get_barrier_semaphore()
    for off in range(1, n):
        pl.semaphore_signal(barrier, inc=1, device_id={"ctx": lax.rem(z + off, n)}, device_id_type=MESH)
    pl.semaphore_signal(barrier, inc=1, device_id={"chan": sibling}, device_id_type=MESH)
    for o in range(1, half):
        pl.semaphore_signal(barrier, inc=1, device_id={"chan": far(o)}, device_id_type=MESH)

    quarter = length // 4

    def proj_copy(comp, piece):
        token = pl.ds(piece * quarter, quarter)
        return pltpu.make_async_copy(
            proj_hbm.at[comp, token, :], proj.at[comp, token, :], proj_sem.at[comp, piece]
        )

    small = [
        pltpu.make_async_copy(source, target, small_sem.at[index])
        for index, (source, target) in enumerate(
            ((dr_hbm, dr_ref), (re_hbm, re_ref), (sf_hbm, sf_ref), (sg_hbm, sg_ref))
        )
    ]
    for piece in range(4):
        for comp in (1, 2):
            proj_copy(comp, piece).start()
        small[piece].start()
    for piece in range(4):
        proj_copy(0, piece).start()

    def w_copy(o, who):
        target = lax.rem(hi + o, half) * 2 + (lo if who else 1 - lo)
        columns = pl.ds(pl.multiple_of(target * out_w, LANES), out_w)
        slot = 2 * o + who
        return pltpu.make_async_copy(w_hbm.at[:, columns], wv.at[slot], w_sem.at[slot])

    if blocks < SUB:
        for buffer in (sft, dec, res, skip, x):
            buffer[...] = jnp.zeros_like(buffer)

    def relay(comp, piece):
        proj_copy(comp, piece).wait()

        @pl.loop(piece * quarter // STEP, (piece + 1) * quarter // STEP)
        def _(i):
            t = pl.multiple_of(i * STEP, STEP)
            for j in range(blocks):
                value = proj[comp, pl.ds(t, STEP), pl.ds(j * LANES, LANES)].astype(jnp.float32)
                x[comp, pl.ds((t + 2) * SUB + j, STEP, stride=SUB), :] = value

    for piece in range(4):
        relay(1, piece)
        relay(2, piece)

    def edge(index, comp, count):
        return pltpu.make_async_remote_copy(
            src_ref=x.at[pl.ds(comp, count), pl.ds(length * SUB, 2 * SUB), :],
            dst_ref=x.at[pl.ds(comp, count), pl.ds(0, 2 * SUB), :],
            send_sem=edge_send.at[index],
            recv_sem=edge_recv.at[index],
            device_id={"ctx": lax.rem(z + 1, n)},
            device_id_type=MESH,
        )

    pl.semaphore_wait(barrier, (n - 1) + 1 + (half - 1))

    @pl.when(z < n - 1)
    def _():
        edge(0, 1, 2).start()

    for o in list(range(1, half)) + [0]:
        for who in range(2):
            w_copy(o, who).start()

    for copy in small:
        copy.wait()
    for j in range(blocks):
        lanes = pl.ds(j * LANES, LANES)
        dec[pl.ds(j, modes, stride=SUB), :] = dr_ref[:, lanes]
        res[pl.ds(j, modes, stride=SUB), :] = re_ref[:, lanes]
        skip[pl.ds(j, 1), :] = sg_ref[:, lanes]
        for comp in range(3):
            sft[pl.ds(comp * 3 * SUB + j, 3, stride=SUB), :] = sf_ref[comp, :, lanes]
    rate = dec[...]
    decay[...] = jnp.exp(-rate)
    first_pow[...] = jnp.exp(-rate * float(length - 2))

    def mode(ref, k):
        return ref[pl.ds(k * SUB, SUB), :]

    def short(comp, t, count):
        total = None
        for lag in range(3):
            value = x[comp, rows(t + 2 - lag, count), :].reshape(count, SUB, LANES)
            value = mode(sft, comp * 3 + lag)[None] * value
            total = value if total is None else total + value
        return total

    def mix(t, count):
        gated = (short(1, t, count) * short(2, t, count)).astype(jnp.bfloat16).astype(jnp.float32)
        g[rows(t, count), :] = gated.reshape(count * SUB, LANES)
        return gated

    once = [mode(decay, k) for k in range(modes)]
    twice = [value * value for value in once]

    def horner(state, gated, count):
        for s in range(0, count, 2):
            state = [
                twice[k] * state[k] + (once[k] * gated[s] + gated[s + 1]) for k in range(modes)
            ]
        return state

    state = horner([jnp.zeros((SUB, LANES), jnp.float32)] * modes, mix(2, SUB - 2), SUB - 2)

    def own_lap(i, state):
        return tuple(horner(list(state), mix(i * SUB, SUB), SUB))

    state = list(lax.fori_loop(1, length // SUB, own_lap, tuple(state)))

    @pl.when(z == 0)
    def _():
        x[:, pl.ds(0, 2 * SUB), :] = jnp.zeros((3, 2 * SUB, LANES), jnp.float32)

    @pl.when(z > 0)
    def _():
        edge(0, 1, 2).wait_recv()

    head = mix(0, 2)
    for k in range(0, modes, 2):
        pair = [state[k + e] + mode(first_pow, k + e) * (once[k + e] * head[0] + head[1]) for e in range(2)]
        own[pl.ds(k * SUB, 2 * SUB), :] = jnp.concatenate(pair, axis=0).astype(jnp.bfloat16)

    def send_state(off):
        return pltpu.make_async_remote_copy(
            src_ref=own,
            dst_ref=arrived.at[off - 1],
            send_sem=state_send.at[off - 1],
            recv_sem=state_recv.at[off - 1],
            device_id={"ctx": lax.rem(z + off, n)},
            device_id_type=MESH,
        )

    for off in range(1, n):

        @pl.when(z + off < n)
        def _(off=off):
            send_state(off).start()

    for piece in range(4):
        relay(0, piece)

    @pl.when(z < n - 1)
    def _():
        edge(1, 0, 1).start()

    gain[...] = res[...] * jnp.sqrt(-expm1(-2.0 * rate))
    passing[...] = jnp.exp(-rate * float(length))
    scale = [mode(gain, k) for k in range(modes)]
    direct = skip[...]

    def near_lap(i, state):
        state = list(state)
        for s in range(SUB):
            token = rows(i * SUB + s)
            gated = g[token, :]
            sums = [direct * gated, None, None, None]
            for k in range(modes):
                state[k] = once[k] * state[k] + gated
                term = scale[k] * state[k]
                sums[k % 4] = term if sums[k % 4] is None else sums[k % 4] + term
            y[token, :] = (sums[0] + sums[1]) + (sums[2] + sums[3])
        return tuple(state)

    lax.fori_loop(
        0, length // SUB, near_lap, tuple(jnp.zeros((SUB, LANES), jnp.float32) for _ in range(modes))
    )

    @pl.when(z > 0)
    def _():
        edge(1, 0, 1).wait_recv()

    @pl.loop(0, length // STEP)
    def _(i):
        t = i * STEP
        q[rows(t, STEP), :] = short(0, t, STEP).reshape(STEP * SUB, LANES)

    carried[...] = jnp.zeros_like(carried)
    for off in range(n - 1, 0, -1):

        @pl.when(z >= off)
        def _(off=off):
            send_state(off).wait_recv()
            carried[...] = carried[...] * passing[...] + arrived[off - 1].astype(jnp.float32)

    reach = [mode(carried, k) * scale[k] * once[k] for k in range(modes)]

    def finish_lap(i, reach):
        reach = list(reach)
        for s in range(SUB):
            token = rows(i * SUB + s)
            sums = [y[token, :], None, None, None]
            for k in range(modes):
                sums[k % 4] = reach[k] if sums[k % 4] is None else sums[k % 4] + reach[k]
                reach[k] = reach[k] * once[k]
            y[token, :] = q[token, :] * ((sums[0] + sums[1]) + (sums[2] + sums[3]))
        return tuple(reach)

    def gather_lap(i):
        t = pl.multiple_of(i * STEP, STEP)
        for j in range(blocks):
            piece = y[pl.ds(t * SUB + j, STEP, stride=SUB), :]
            mo[pl.ds(t, STEP), pl.ds(j * LANES, LANES)] = piece.astype(jnp.bfloat16)

    def to_sibling(o, p):
        token = pl.ds(*parts[p])
        return pltpu.make_async_remote_copy(
            src_ref=ss.at[o, token, :],
            dst_ref=sr.at[o, token, :],
            send_sem=sib_send.at[o, p],
            recv_sem=sib_recv.at[o, p],
            device_id={"chan": sibling},
            device_id_type=MESH,
        )

    def to_far(o, p):
        token = pl.ds(*parts[p])
        return pltpu.make_async_remote_copy(
            src_ref=xs.at[o - 1, token, :],
            dst_ref=xr.at[o - 1, token, :],
            send_sem=far_send.at[o - 1, p],
            recv_sem=far_recv.at[o - 1, p],
            device_id={"chan": far(o)},
            device_id_type=MESH,
        )

    order = list(range(1, half)) + [0]
    for p, (start, count) in enumerate(parts):
        token = pl.ds(start, count)
        reach = list(lax.fori_loop(start // SUB, (start + count) // SUB, finish_lap, tuple(reach)))
        pl.loop(start // STEP, (start + count) // STEP)(gather_lap)

        def product(slot):
            return jnp.dot(mo[token, :], wv[slot], preferred_element_type=jnp.float32)

        for o in order:
            for who in range(2):
                if p == 0:
                    w_copy(o, who).wait()
                if who == 0:
                    ss[o, token, :] = product(2 * o).astype(jnp.bfloat16)
                    to_sibling(o, p).start()
                else:
                    acc[o, token, :] = product(2 * o + 1)
        for o in range(1, half):
            to_sibling(o, p).wait_recv()
            xs[o - 1, token, :] = (acc[o, token, :] + sr[o, token, :].astype(jnp.float32)).astype(jnp.bfloat16)
            to_far(o, p).start()

    for p, (start, count) in enumerate(parts):
        token = pl.ds(start, count)
        to_sibling(0, p).wait_recv()
        total = acc[0, token, :] + sr[0, token, :].astype(jnp.float32)
        for o in range(1, half):
            to_far(o, p).wait_recv()
            total = total + xr[o - 1, token, :].astype(jnp.float32)
        out_ref[token, :] = total.astype(out_ref.dtype)

    @pl.when(z < n - 1)
    def _():
        edge(0, 1, 2).wait_send()
        edge(1, 0, 1).wait_send()

    for off in range(1, n):

        @pl.when(z + off < n)
        def _(off=off):
            send_state(off).wait_send()

    for p in range(len(parts)):
        for o in range(half):
            to_sibling(o, p).wait_send()
        for o in range(1, half):
            to_far(o, p).wait_send()


def body(projected, short_filter, decay_rates, residues, skip_gain, out_weight):
    n, m = lax.axis_size("ctx"), lax.axis_size("chan")
    length, width = projected.shape[1:]
    modes = decay_rates.shape[0]
    out_w = out_weight.shape[1] // m
    half = m // 2
    count = len(parts_of(length))
    f32, bf16 = jnp.float32, jnp.bfloat16
    table = pltpu.VMEM((modes * SUB, LANES), f32)
    tokens = pltpu.VMEM((length * SUB, LANES), f32)
    dma = pltpu.SemaphoreType.DMA
    vmem = pl.BlockSpec(memory_space=pltpu.VMEM)
    hbm = pl.BlockSpec(memory_space=pltpu.HBM)
    return pl.pallas_call(
        functools.partial(kernel, n, m),
        out_shape=jax.ShapeDtypeStruct((length, out_w), bf16),
        in_specs=[hbm] * 6,
        out_specs=vmem,
        scratch_shapes=[
            pltpu.VMEM((3, length, width), bf16),
            pltpu.VMEM(short_filter.shape, f32),
            pltpu.VMEM(decay_rates.shape, f32),
            pltpu.VMEM(residues.shape, f32),
            pltpu.VMEM((1, width), f32),
            pltpu.VMEM((m, width, out_w), bf16),
            pltpu.VMEM((9 * SUB, LANES), f32),
            table,
            table,
            pltpu.VMEM((SUB, LANES), f32),
            table,
            table,
            table,
            table,
            pltpu.VMEM((3, (length + 2) * SUB, LANES), f32),
            tokens,
            tokens,
            tokens,
            pltpu.VMEM((length, width), bf16),
            pltpu.VMEM((modes * SUB, LANES), bf16),
            pltpu.VMEM((n - 1, modes * SUB, LANES), bf16),
            table,
            pltpu.VMEM((half, length, out_w), bf16),
            pltpu.VMEM((half, length, out_w), bf16),
            pltpu.VMEM((half - 1, length, out_w), bf16),
            pltpu.VMEM((half - 1, length, out_w), bf16),
            pltpu.VMEM((half, length, out_w), f32),
            dma((3, 4)),
            dma((4,)),
            dma((m,)),
            dma((2,)),
            dma((2,)),
            dma((n - 1,)),
            dma((n - 1,)),
            dma((half, count)),
            dma((half, count)),
            dma((half - 1, count)),
            dma((half - 1, count)),
        ],
        compiler_params=pltpu.CompilerParams(
            collective_id=0, has_side_effects=True, vmem_limit_bytes=62 * 1024 * 1024
        ),
        cost_estimate=pl.CostEstimate(
            flops=2 * length * width * out_w * m, bytes_accessed=2 * width * out_w * m, transcendentals=0
        ),
        name="hyena_layer",
    )(projected, short_filter, decay_rates, residues, skip_gain.reshape(1, width), out_weight)


def solution(mesh):
    in_specs = (
        P(None, ("groups", "ctx"), "chan"),
        P(None, None, "chan"),
        P(None, "chan"),
        P(None, "chan"),
        P("chan"),
        P("chan", None),
    )
    out_specs = P(("groups", "ctx"), "chan")
    return jax.shard_map(body, mesh=mesh, in_specs=in_specs, out_specs=out_specs, check_vma=False)
```

```python
import functools

import jax
import jax.numpy as jnp
from jax import lax
from jax.experimental import pallas as pl
from jax.experimental.pallas import tpu as pltpu
from jax.sharding import PartitionSpec as P

MESH = pl.DeviceIdType.MESH
LANES = 128
SUB = 8
STEP = 16


def parts_of(length):
    return [(0, length // 4), (length // 4, length // 4), (length // 2, length // 2)]


def expm1(v):
    series = jnp.ones_like(v)
    for order in range(9, 1, -1):
        series = 1.0 + series * v * (1.0 / order)
    return jnp.where(v > -0.3, v * series, jnp.exp(v) - 1.0)


def rows(token, count=1):
    start = token * SUB
    if not isinstance(start, int):
        start = pl.multiple_of(start, SUB)
    return pl.ds(start, count * SUB)


def kernel(
    n, m, proj_hbm, sf_hbm, dr_hbm, re_hbm, sg_hbm, w_hbm, out_ref,
    proj, sf_ref, dr_ref, re_ref, sg_ref, wv, sft, dec, res, skip, decay, gain, passing, first_pow,
    x, q, g, y, mo, own, arrived, carried, ss, sr, xs, xr, acc,
    proj_sem, small_sem, w_sem, edge_send, edge_recv, state_send, state_recv,
    sib_send, sib_recv, far_send, far_recv,
):
    length, width = proj.shape[1:]
    modes = dr_ref.shape[0]
    blocks = width // LANES
    half = m // 2
    out_w = out_ref.shape[1]
    parts = parts_of(length)
    z, c = lax.axis_index("ctx"), lax.axis_index("chan")
    hi, lo = c // 2, lax.rem(c, 2)
    sibling = hi * 2 + (1 - lo)

    def far(o):
        return lax.rem(hi + o, half) * 2 + lo

    barrier = pltpu.get_barrier_semaphore()
    for off in range(1, n):
        pl.semaphore_signal(barrier, inc=1, device_id={"ctx": lax.rem(z + off, n)}, device_id_type=MESH)
    pl.semaphore_signal(barrier, inc=1, device_id={"chan": sibling}, device_id_type=MESH)
    for o in range(1, half):
        pl.semaphore_signal(barrier, inc=1, device_id={"chan": far(o)}, device_id_type=MESH)

    quarter = length // 4

    def proj_copy(comp, piece):
        token = pl.ds(piece * quarter, quarter)
        return pltpu.make_async_copy(
            proj_hbm.at[comp, token, :], proj.at[comp, token, :], proj_sem.at[comp, piece]
        )

    small = [
        pltpu.make_async_copy(source, target, small_sem.at[index])
        for index, (source, target) in enumerate(
            ((dr_hbm, dr_ref), (re_hbm, re_ref), (sf_hbm, sf_ref), (sg_hbm, sg_ref))
        )
    ]
    for piece in range(4):
        for comp in (1, 2):
            proj_copy(comp, piece).start()
        small[piece].start()
    for piece in range(4):
        proj_copy(0, piece).start()

    def w_copy(o, who):
        target = lax.rem(hi + o, half) * 2 + (lo if who else 1 - lo)
        columns = pl.ds(pl.multiple_of(target * out_w, LANES), out_w)
        slot = 2 * o + who
        return pltpu.make_async_copy(w_hbm.at[:, columns], wv.at[slot], w_sem.at[slot])

    if blocks < SUB:
        for buffer in (sft, dec, res, skip, x):
            buffer[...] = jnp.zeros_like(buffer)

    span = blocks * STEP

    def permutation(height, depth, source):
        row = lax.broadcasted_iota(jnp.int32, (height, depth), 0)
        column = lax.broadcasted_iota(jnp.int32, (height, depth), 1)
        return jnp.where(source(row) == column, 1.0, 0.0).astype(jnp.bfloat16)

    to_token = permutation(STEP * SUB, span, lambda row: (row % SUB) * STEP + row // SUB)
    to_block = permutation(span, STEP * SUB, lambda row: (row % STEP) * SUB + row // STEP)

    def relay(comps, piece):
        for comp in comps:
            proj_copy(comp, piece).wait()
        for t in range(piece * quarter, (piece + 1) * quarter, STEP):
            stacked = [
                jnp.concatenate(
                    [proj[comp, pl.ds(t, STEP), pl.ds(j * LANES, LANES)] for j in range(blocks)], axis=0
                )
                for comp in comps
            ]
            moved = jnp.dot(
                to_token, jnp.concatenate(stacked, axis=1), preferred_element_type=jnp.float32
            )
            for index, comp in enumerate(comps):
                x[comp, rows(t + 2, STEP), :] = moved[:, index * LANES : (index + 1) * LANES]

    for piece in range(4):
        relay((1, 2), piece)

    def edge(index, comp, count):
        return pltpu.make_async_remote_copy(
            src_ref=x.at[pl.ds(comp, count), pl.ds(length * SUB, 2 * SUB), :],
            dst_ref=x.at[pl.ds(comp, count), pl.ds(0, 2 * SUB), :],
            send_sem=edge_send.at[index],
            recv_sem=edge_recv.at[index],
            device_id={"ctx": lax.rem(z + 1, n)},
            device_id_type=MESH,
        )

    pl.semaphore_wait(barrier, (n - 1) + 1 + (half - 1))

    @pl.when(z < n - 1)
    def _():
        edge(0, 1, 2).start()

    for o in list(range(1, half)) + [0]:
        for who in range(2):
            w_copy(o, who).start()

    for copy in small:
        copy.wait()
    for j in range(blocks):
        lanes = pl.ds(j * LANES, LANES)
        dec[pl.ds(j, modes, stride=SUB), :] = dr_ref[:, lanes]
        res[pl.ds(j, modes, stride=SUB), :] = re_ref[:, lanes]
        skip[pl.ds(j, 1), :] = sg_ref[:, lanes]
        for comp in range(3):
            sft[pl.ds(comp * 3 * SUB + j, 3, stride=SUB), :] = sf_ref[comp, :, lanes]
    rate = dec[...]
    decay[...] = jnp.exp(-rate)
    first_pow[...] = jnp.exp(-rate * float(length - 2))

    def mode(ref, k):
        return ref[pl.ds(k * SUB, SUB), :]

    def short(comp, t, count):
        total = None
        for lag in range(3):
            value = x[comp, rows(t + 2 - lag, count), :].reshape(count, SUB, LANES)
            value = mode(sft, comp * 3 + lag)[None] * value
            total = value if total is None else total + value
        return total

    def mix(t, count):
        gated = (short(1, t, count) * short(2, t, count)).astype(jnp.bfloat16).astype(jnp.float32)
        g[rows(t, count), :] = gated.reshape(count * SUB, LANES)
        return gated

    once = [mode(decay, k) for k in range(modes)]
    twice = [value * value for value in once]

    def horner(state, gated, count):
        for s in range(0, count, 2):
            state = [
                twice[k] * state[k] + (once[k] * gated[s] + gated[s + 1]) for k in range(modes)
            ]
        return state

    state = horner([jnp.zeros((SUB, LANES), jnp.float32)] * modes, mix(2, SUB - 2), SUB - 2)

    def own_lap(i, state):
        return tuple(horner(list(state), mix(i * SUB, SUB), SUB))

    state = list(lax.fori_loop(1, length // SUB, own_lap, tuple(state)))

    @pl.when(z == 0)
    def _():
        x[:, pl.ds(0, 2 * SUB), :] = jnp.zeros((3, 2 * SUB, LANES), jnp.float32)

    @pl.when(z > 0)
    def _():
        edge(0, 1, 2).wait_recv()

    head = mix(0, 2)
    for k in range(0, modes, 2):
        pair = [state[k + e] + mode(first_pow, k + e) * (once[k + e] * head[0] + head[1]) for e in range(2)]
        own[pl.ds(k * SUB, 2 * SUB), :] = jnp.concatenate(pair, axis=0).astype(jnp.bfloat16)

    def send_state(off):
        return pltpu.make_async_remote_copy(
            src_ref=own,
            dst_ref=arrived.at[off - 1],
            send_sem=state_send.at[off - 1],
            recv_sem=state_recv.at[off - 1],
            device_id={"ctx": lax.rem(z + off, n)},
            device_id_type=MESH,
        )

    for off in range(1, n):

        @pl.when(z + off < n)
        def _(off=off):
            send_state(off).start()

    for piece in range(4):
        relay((0,), piece)

    @pl.when(z < n - 1)
    def _():
        edge(1, 0, 1).start()

    gain[...] = res[...] * jnp.sqrt(-expm1(-2.0 * rate))
    passing[...] = jnp.exp(-rate * float(length))
    scale = [mode(gain, k) for k in range(modes)]
    direct = skip[...]

    def near_lap(i, state):
        state = list(state)
        for s in range(SUB):
            token = rows(i * SUB + s)
            gated = g[token, :]
            sums = [direct * gated, None, None, None]
            for k in range(modes):
                state[k] = once[k] * state[k] + gated
                term = scale[k] * state[k]
                sums[k % 4] = term if sums[k % 4] is None else sums[k % 4] + term
            y[token, :] = (sums[0] + sums[1]) + (sums[2] + sums[3])
        return tuple(state)

    lax.fori_loop(
        0, length // SUB, near_lap, tuple(jnp.zeros((SUB, LANES), jnp.float32) for _ in range(modes))
    )

    @pl.when(z > 0)
    def _():
        edge(1, 0, 1).wait_recv()

    @pl.loop(0, length // STEP)
    def _(i):
        t = i * STEP
        q[rows(t, STEP), :] = short(0, t, STEP).reshape(STEP * SUB, LANES)

    carried[...] = jnp.zeros_like(carried)
    for off in range(n - 1, 0, -1):

        @pl.when(z >= off)
        def _(off=off):
            send_state(off).wait_recv()
            carried[...] = carried[...] * passing[...] + arrived[off - 1].astype(jnp.float32)

    reach = [mode(carried, k) * scale[k] * once[k] for k in range(modes)]

    def finish_lap(i, reach):
        reach = list(reach)
        for s in range(SUB):
            token = rows(i * SUB + s)
            sums = [y[token, :], None, None, None]
            for k in range(modes):
                sums[k % 4] = reach[k] if sums[k % 4] is None else sums[k % 4] + reach[k]
                reach[k] = reach[k] * once[k]
            y[token, :] = q[token, :] * ((sums[0] + sums[1]) + (sums[2] + sums[3]))
        return tuple(reach)

    def gather(start):
        groups = [
            y[rows(start + e * STEP, STEP), :].astype(jnp.bfloat16) for e in range(quarter // STEP)
        ]
        moved = jnp.dot(
            to_block, jnp.concatenate(groups, axis=1), preferred_element_type=jnp.float32
        ).astype(jnp.bfloat16)
        for e in range(quarter // STEP):
            for j in range(blocks):
                mo[pl.ds(start + e * STEP, STEP), pl.ds(j * LANES, LANES)] = moved[
                    j * STEP : (j + 1) * STEP, e * LANES : (e + 1) * LANES
                ]

    def to_sibling(o, p):
        token = pl.ds(*parts[p]) if o else pl.ds(0, length)
        return pltpu.make_async_remote_copy(
            src_ref=ss.at[o, token, :],
            dst_ref=sr.at[o, token, :],
            send_sem=sib_send.at[o, p],
            recv_sem=sib_recv.at[o, p],
            device_id={"chan": sibling},
            device_id_type=MESH,
        )

    def to_far(o, p):
        token = pl.ds(*parts[p])
        return pltpu.make_async_remote_copy(
            src_ref=xs.at[o - 1, token, :],
            dst_ref=xr.at[o - 1, token, :],
            send_sem=far_send.at[o - 1, p],
            recv_sem=far_recv.at[o - 1, p],
            device_id={"chan": far(o)},
            device_id_type=MESH,
        )

    def product(token, slot):
        return jnp.dot(mo[token, :], wv[slot], preferred_element_type=jnp.float32)

    def forward(p):
        token = pl.ds(*parts[p])
        for o in range(1, half):
            to_sibling(o, p).wait_recv()
            xs[o - 1, token, :] = (acc[o, token, :] + sr[o, token, :].astype(jnp.float32)).astype(jnp.bfloat16)
            to_far(o, p).start()

    for p, (start, count) in enumerate(parts):
        token = pl.ds(start, count)
        reach = list(lax.fori_loop(start // SUB, (start + count) // SUB, finish_lap, tuple(reach)))
        for first in range(start, start + count, quarter):
            gather(first)
        if p > 0:
            forward(p - 1)
        for o in range(1, half):
            if p == 0:
                w_copy(o, 0).wait()
            ss[o, token, :] = product(token, 2 * o).astype(jnp.bfloat16)
            to_sibling(o, p).start()
        for o in range(1, half):
            if p == 0:
                w_copy(o, 1).wait()
            acc[o, token, :] = product(token, 2 * o + 1)

    every = pl.ds(0, length)
    w_copy(0, 0).wait()
    ss[0] = product(every, 0).astype(jnp.bfloat16)
    to_sibling(0, 0).start()
    forward(len(parts) - 1)
    w_copy(0, 1).wait()
    acc[0] = product(every, 1)
    to_sibling(0, 0).wait_recv()
    for p, (start, count) in enumerate(parts):
        token = pl.ds(start, count)
        total = acc[0, token, :] + sr[0, token, :].astype(jnp.float32)
        for o in range(1, half):
            to_far(o, p).wait_recv()
            total = total + xr[o - 1, token, :].astype(jnp.float32)
        out_ref[token, :] = total.astype(out_ref.dtype)

    @pl.when(z < n - 1)
    def _():
        edge(0, 1, 2).wait_send()
        edge(1, 0, 1).wait_send()

    for off in range(1, n):

        @pl.when(z + off < n)
        def _(off=off):
            send_state(off).wait_send()

    to_sibling(0, 0).wait_send()
    for p in range(len(parts)):
        for o in range(1, half):
            to_sibling(o, p).wait_send()
            to_far(o, p).wait_send()


def body(projected, short_filter, decay_rates, residues, skip_gain, out_weight):
    n, m = lax.axis_size("ctx"), lax.axis_size("chan")
    length, width = projected.shape[1:]
    modes = decay_rates.shape[0]
    out_w = out_weight.shape[1] // m
    half = m // 2
    count = len(parts_of(length))
    f32, bf16 = jnp.float32, jnp.bfloat16
    table = pltpu.VMEM((modes * SUB, LANES), f32)
    tokens = pltpu.VMEM((length * SUB, LANES), f32)
    dma = pltpu.SemaphoreType.DMA
    vmem = pl.BlockSpec(memory_space=pltpu.VMEM)
    hbm = pl.BlockSpec(memory_space=pltpu.HBM)
    return pl.pallas_call(
        functools.partial(kernel, n, m),
        out_shape=pltpu.VMEM((length, out_w), bf16),
        in_specs=[hbm] * 6,
        out_specs=vmem,
        scratch_shapes=[
            pltpu.VMEM((3, length, width), bf16),
            pltpu.VMEM(short_filter.shape, f32),
            pltpu.VMEM(decay_rates.shape, f32),
            pltpu.VMEM(residues.shape, f32),
            pltpu.VMEM((1, width), f32),
            pltpu.VMEM((m, width, out_w), bf16),
            pltpu.VMEM((9 * SUB, LANES), f32),
            table,
            table,
            pltpu.VMEM((SUB, LANES), f32),
            table,
            table,
            table,
            table,
            pltpu.VMEM((3, (length + 2) * SUB, LANES), f32),
            tokens,
            tokens,
            tokens,
            pltpu.VMEM((length, width), bf16),
            pltpu.VMEM((modes * SUB, LANES), bf16),
            pltpu.VMEM((n - 1, modes * SUB, LANES), bf16),
            table,
            pltpu.VMEM((half, length, out_w), bf16),
            pltpu.VMEM((half, length, out_w), bf16),
            pltpu.VMEM((half - 1, length, out_w), bf16),
            pltpu.VMEM((half - 1, length, out_w), bf16),
            pltpu.VMEM((half, length, out_w), f32),
            dma((3, 4)),
            dma((4,)),
            dma((m,)),
            dma((2,)),
            dma((2,)),
            dma((n - 1,)),
            dma((n - 1,)),
            dma((half, count)),
            dma((half, count)),
            dma((half - 1, count)),
            dma((half - 1, count)),
        ],
        compiler_params=pltpu.CompilerParams(
            collective_id=0, has_side_effects=True, vmem_limit_bytes=60 * 1024 * 1024
        ),
        cost_estimate=pl.CostEstimate(
            flops=2 * length * width * out_w * m, bytes_accessed=2 * width * out_w * m, transcendentals=0
        ),
        name="hyena_layer",
    )(projected, short_filter, decay_rates, residues, skip_gain.reshape(1, width), out_weight)


def solution(mesh):
    in_specs = (
        P(None, ("groups", "ctx"), "chan"),
        P(None, None, "chan"),
        P(None, "chan"),
        P(None, "chan"),
        P("chan"),
        P("chan", None),
    )
    out_specs = P(("groups", "ctx"), "chan")
    return jax.shard_map(body, mesh=mesh, in_specs=in_specs, out_specs=out_specs, check_vma=False)
```

```python
import functools

import jax
import jax.numpy as jnp
from jax import lax
from jax.experimental import pallas as pl
from jax.experimental.pallas import tpu as pltpu
from jax.sharding import PartitionSpec as P

MESH = pl.DeviceIdType.MESH
LANES = 128
SUB = 8
STEP = 16


def parts_of(length):
    return [(0, length // 4), (length // 4, length // 4), (length // 2, length // 2)]


def expm1(v):
    series = jnp.ones_like(v)
    for order in range(9, 1, -1):
        series = 1.0 + series * v * (1.0 / order)
    return jnp.where(v > -0.3, v * series, jnp.exp(v) - 1.0)


def rows(token, count=1):
    start = token * SUB
    if not isinstance(start, int):
        start = pl.multiple_of(start, SUB)
    return pl.ds(start, count * SUB)


def kernel(
    n, m, proj_hbm, sf_hbm, dr_hbm, re_hbm, sg_hbm, w_hbm, out_ref,
    proj, sf_ref, dr_ref, re_ref, sg_ref, wv, sft, dec, res, skip, decay, gain, passing, first_pow,
    x, q, g, y, mo, own, arrived, carried, ss, sr, xs, xr, acc,
    proj_sem, small_sem, w_sem, edge_send, edge_recv, state_send, state_recv,
    sib_send, sib_recv, far_send, far_recv,
):
    length, width = proj.shape[1:]
    modes = dr_ref.shape[0]
    blocks = width // LANES
    half = m // 2
    out_w = out_ref.shape[1]
    parts = parts_of(length)
    z, c = lax.axis_index("ctx"), lax.axis_index("chan")
    hi, lo = c // 2, lax.rem(c, 2)
    sibling = hi * 2 + (1 - lo)

    def far(o):
        return lax.rem(hi + o, half) * 2 + lo

    barrier = pltpu.get_barrier_semaphore()
    for off in range(1, n):
        pl.semaphore_signal(barrier, inc=1, device_id={"ctx": lax.rem(z + off, n)}, device_id_type=MESH)
    pl.semaphore_signal(barrier, inc=1, device_id={"chan": sibling}, device_id_type=MESH)
    for o in range(1, half):
        pl.semaphore_signal(barrier, inc=1, device_id={"chan": far(o)}, device_id_type=MESH)

    quarter = length // 4

    def proj_copy(comp, piece):
        token = pl.ds(piece * quarter, quarter)
        return pltpu.make_async_copy(
            proj_hbm.at[comp, token, :], proj.at[comp, token, :], proj_sem.at[comp, piece]
        )

    small = [
        pltpu.make_async_copy(source, target, small_sem.at[index])
        for index, (source, target) in enumerate(
            ((dr_hbm, dr_ref), (sf_hbm, sf_ref), (re_hbm, re_ref), (sg_hbm, sg_ref))
        )
    ]
    for index, piece in enumerate((3, 0, 1, 2)):
        for comp in (1, 2):
            proj_copy(comp, piece).start()
        small[index].start()
    for piece in (3, 0, 1, 2):
        proj_copy(0, piece).start()

    def w_copy(o, who):
        target = lax.rem(hi + o, half) * 2 + (lo if who else 1 - lo)
        columns = pl.ds(pl.multiple_of(target * out_w, LANES), out_w)
        slot = 2 * o + who
        return pltpu.make_async_copy(w_hbm.at[:, columns], wv.at[slot], w_sem.at[slot])

    if blocks < SUB:
        for buffer in (sft, dec, res, skip, x):
            buffer[...] = jnp.zeros_like(buffer)

    span = blocks * STEP

    def permutation(height, depth, source):
        row = lax.broadcasted_iota(jnp.int32, (height, depth), 0)
        column = lax.broadcasted_iota(jnp.int32, (height, depth), 1)
        return jnp.where(source(row) == column, 1.0, 0.0).astype(jnp.bfloat16)

    to_token = permutation(STEP * SUB, span, lambda row: (row % SUB) * STEP + row // SUB)
    to_block = permutation(span, STEP * SUB, lambda row: (row % STEP) * SUB + row // STEP)

    def relay(comps, piece):
        for comp in comps:
            proj_copy(comp, piece).wait()
        for t in range(piece * quarter, (piece + 1) * quarter, STEP):
            stacked = [
                jnp.concatenate(
                    [proj[comp, pl.ds(t, STEP), pl.ds(j * LANES, LANES)] for j in range(blocks)], axis=0
                )
                for comp in comps
            ]
            moved = jnp.dot(
                to_token, jnp.concatenate(stacked, axis=1), preferred_element_type=jnp.float32
            )
            for index, comp in enumerate(comps):
                x[comp, rows(t + 2, STEP), :] = moved[:, index * LANES : (index + 1) * LANES]

    relay((1, 2), 3)

    def edge(index, comp, count):
        return pltpu.make_async_remote_copy(
            src_ref=x.at[pl.ds(comp, count), pl.ds(length * SUB, 2 * SUB), :],
            dst_ref=x.at[pl.ds(comp, count), pl.ds(0, 2 * SUB), :],
            send_sem=edge_send.at[index],
            recv_sem=edge_recv.at[index],
            device_id={"ctx": lax.rem(z + 1, n)},
            device_id_type=MESH,
        )

    pl.semaphore_wait(barrier, (n - 1) + 1 + (half - 1))

    @pl.when(z < n - 1)
    def _():
        edge(0, 1, 2).start()

    for o in list(range(1, half)) + [0]:
        for who in range(2):
            w_copy(o, who).start()

    for copy in small:
        copy.wait()
    for j in range(blocks):
        lanes = pl.ds(j * LANES, LANES)
        dec[pl.ds(j, modes, stride=SUB), :] = dr_ref[:, lanes]
        res[pl.ds(j, modes, stride=SUB), :] = re_ref[:, lanes]
        skip[pl.ds(j, 1), :] = sg_ref[:, lanes]
        for comp in range(3):
            sft[pl.ds(comp * 3 * SUB + j, 3, stride=SUB), :] = sf_ref[comp, :, lanes]
    rate = dec[...]
    decay[...] = jnp.exp(-rate)
    first_pow[...] = jnp.exp(-rate * float(length - 2))

    def mode(ref, k):
        return ref[pl.ds(k * SUB, SUB), :]

    def short(comp, t, count):
        total = None
        for lag in range(3):
            value = x[comp, rows(t + 2 - lag, count), :].reshape(count, SUB, LANES)
            value = mode(sft, comp * 3 + lag)[None] * value
            total = value if total is None else total + value
        return total

    def mix(t, count):
        gated = (short(1, t, count) * short(2, t, count)).astype(jnp.bfloat16).astype(jnp.float32)
        g[rows(t, count), :] = gated.reshape(count * SUB, LANES)
        return gated

    once = [mode(decay, k) for k in range(modes)]
    twice = [value * value for value in once]

    def horner(group, state, gated, count):
        for s in range(0, count, 2):
            state = [
                twice[k] * value + (once[k] * gated[s] + gated[s + 1]) for k, value in zip(group, state)
            ]
        return state

    zero = jnp.zeros((SUB, LANES), jnp.float32)
    groups = [range(0, modes // 2), range(modes // 2, modes)]

    def own_lap(i, state):
        return tuple(horner(groups[0], list(state), mix(i * SUB, SUB), SUB))

    relay((1, 2), 0)
    state = horner(groups[0], [zero] * len(groups[0]), mix(2, SUB - 2), SUB - 2)
    for piece in range(4):
        if piece in (1, 2):
            relay((1, 2), piece)
        first = max(1, piece * quarter // SUB)
        state = list(lax.fori_loop(first, (piece + 1) * quarter // SUB, own_lap, tuple(state)))

    @pl.when(z == 0)
    def _():
        x[:, pl.ds(0, 2 * SUB), :] = jnp.zeros((3, 2 * SUB, LANES), jnp.float32)

    @pl.when(z > 0)
    def _():
        edge(0, 1, 2).wait_recv()

    head = mix(0, 2)

    def send_state(off, part):
        piece = pl.ds(groups[part][0] * SUB, len(groups[part]) * SUB)
        return pltpu.make_async_remote_copy(
            src_ref=own.at[piece, :],
            dst_ref=arrived.at[off - 1, piece, :],
            send_sem=state_send.at[off - 1, part],
            recv_sem=state_recv.at[off - 1, part],
            device_id={"ctx": lax.rem(z + off, n)},
            device_id_type=MESH,
        )

    def publish(part, state):
        group = groups[part]
        whole = [
            value + mode(first_pow, k) * (once[k] * head[0] + head[1]) for k, value in zip(group, state)
        ]
        for index in range(0, len(group), 2):
            pair = jnp.concatenate(whole[index : index + 2], axis=0)
            own[pl.ds(group[index] * SUB, 2 * SUB), :] = pair.astype(jnp.bfloat16)
        for off in range(1, n):

            @pl.when(z + off < n)
            def _(off=off):
                send_state(off, part).start()

    publish(0, state)

    def rest_lap(i, state):
        gated = g[rows(i * SUB, SUB), :].reshape(SUB, SUB, LANES)
        return tuple(horner(groups[1], list(state), gated, SUB))

    gated = g[rows(2, SUB - 2), :].reshape(SUB - 2, SUB, LANES)
    state = horner(groups[1], [zero] * len(groups[1]), gated, SUB - 2)
    publish(1, list(lax.fori_loop(1, length // SUB, rest_lap, tuple(state))))

    for piece in range(4):
        relay((0,), piece)

    @pl.when(z < n - 1)
    def _():
        edge(1, 0, 1).start()

    gain[...] = res[...] * jnp.sqrt(-expm1(-2.0 * rate))
    passing[...] = jnp.exp(-rate * float(length))
    scale = [mode(gain, k) for k in range(modes)]
    direct = skip[...]

    def near_lap(i, state):
        state = list(state)
        for s in range(SUB):
            token = rows(i * SUB + s)
            gated = g[token, :]
            sums = [direct * gated, None, None, None]
            for k in range(modes):
                state[k] = once[k] * state[k] + gated
                term = scale[k] * state[k]
                sums[k % 4] = term if sums[k % 4] is None else sums[k % 4] + term
            y[token, :] = (sums[0] + sums[1]) + (sums[2] + sums[3])
        return tuple(state)

    lax.fori_loop(
        0, length // SUB, near_lap, (zero,) * modes
    )

    @pl.when(z > 0)
    def _():
        edge(1, 0, 1).wait_recv()

    @pl.loop(0, length // STEP)
    def _(i):
        t = i * STEP
        q[rows(t, STEP), :] = short(0, t, STEP).reshape(STEP * SUB, LANES)

    carried[...] = jnp.zeros_like(carried)
    for off in range(n - 1, 0, -1):

        @pl.when(z >= off)
        def _(off=off):
            for part in range(2):
                send_state(off, part).wait_recv()
            carried[...] = carried[...] * passing[...] + arrived[off - 1].astype(jnp.float32)

    reach = [mode(carried, k) * scale[k] * once[k] for k in range(modes)]

    def finish_lap(i, reach):
        reach = list(reach)
        for s in range(SUB):
            token = rows(i * SUB + s)
            sums = [y[token, :], None, None, None]
            for k in range(modes):
                sums[k % 4] = reach[k] if sums[k % 4] is None else sums[k % 4] + reach[k]
                reach[k] = reach[k] * once[k]
            y[token, :] = q[token, :] * ((sums[0] + sums[1]) + (sums[2] + sums[3]))
        return tuple(reach)

    def gather(start):
        columns = [
            y[rows(start + e * STEP, STEP), :].astype(jnp.bfloat16) for e in range(quarter // STEP)
        ]
        moved = jnp.dot(
            to_block, jnp.concatenate(columns, axis=1), preferred_element_type=jnp.float32
        ).astype(jnp.bfloat16)
        for e in range(quarter // STEP):
            for j in range(blocks):
                mo[pl.ds(start + e * STEP, STEP), pl.ds(j * LANES, LANES)] = moved[
                    j * STEP : (j + 1) * STEP, e * LANES : (e + 1) * LANES
                ]

    def to_sibling(o, p):
        token = pl.ds(*parts[p]) if o else pl.ds(0, length)
        return pltpu.make_async_remote_copy(
            src_ref=ss.at[o, token, :],
            dst_ref=sr.at[o, token, :],
            send_sem=sib_send.at[o, p],
            recv_sem=sib_recv.at[o, p],
            device_id={"chan": sibling},
            device_id_type=MESH,
        )

    def to_far(o, p):
        token = pl.ds(*parts[p])
        return pltpu.make_async_remote_copy(
            src_ref=xs.at[o - 1, token, :],
            dst_ref=xr.at[o - 1, token, :],
            send_sem=far_send.at[o - 1, p],
            recv_sem=far_recv.at[o - 1, p],
            device_id={"chan": far(o)},
            device_id_type=MESH,
        )

    def product(token, slot):
        return jnp.dot(mo[token, :], wv[slot], preferred_element_type=jnp.float32)

    def forward(p):
        token = pl.ds(*parts[p])
        for o in range(1, half):
            to_sibling(o, p).wait_recv()
            xs[o - 1, token, :] = (acc[o, token, :] + sr[o, token, :].astype(jnp.float32)).astype(jnp.bfloat16)
            to_far(o, p).start()

    for p, (start, count) in enumerate(parts):
        token = pl.ds(start, count)
        reach = list(lax.fori_loop(start // SUB, (start + count) // SUB, finish_lap, tuple(reach)))
        for first in range(start, start + count, quarter):
            gather(first)
        if p > 0:
            forward(p - 1)
        for o in range(1, half):
            if p == 0:
                w_copy(o, 0).wait()
            ss[o, token, :] = product(token, 2 * o).astype(jnp.bfloat16)
            to_sibling(o, p).start()
        for o in range(1, half):
            if p == 0:
                w_copy(o, 1).wait()
            acc[o, token, :] = product(token, 2 * o + 1)

    every = pl.ds(0, length)
    w_copy(0, 0).wait()
    ss[0] = product(every, 0).astype(jnp.bfloat16)
    to_sibling(0, 0).start()
    forward(len(parts) - 1)
    w_copy(0, 1).wait()
    acc[0] = product(every, 1)
    to_sibling(0, 0).wait_recv()
    for p, (start, count) in enumerate(parts):
        token = pl.ds(start, count)
        total = acc[0, token, :] + sr[0, token, :].astype(jnp.float32)
        for o in range(1, half):
            to_far(o, p).wait_recv()
            total = total + xr[o - 1, token, :].astype(jnp.float32)
        out_ref[token, :] = total.astype(out_ref.dtype)

    @pl.when(z < n - 1)
    def _():
        edge(0, 1, 2).wait_send()
        edge(1, 0, 1).wait_send()

    for off in range(1, n):

        @pl.when(z + off < n)
        def _(off=off):
            for part in range(2):
                send_state(off, part).wait_send()

    to_sibling(0, 0).wait_send()
    for p in range(len(parts)):
        for o in range(1, half):
            to_sibling(o, p).wait_send()
            to_far(o, p).wait_send()


def body(projected, short_filter, decay_rates, residues, skip_gain, out_weight):
    n, m = lax.axis_size("ctx"), lax.axis_size("chan")
    length, width = projected.shape[1:]
    modes = decay_rates.shape[0]
    out_w = out_weight.shape[1] // m
    half = m // 2
    count = len(parts_of(length))
    f32, bf16 = jnp.float32, jnp.bfloat16
    table = pltpu.VMEM((modes * SUB, LANES), f32)
    tokens = pltpu.VMEM((length * SUB, LANES), f32)
    dma = pltpu.SemaphoreType.DMA
    vmem = pl.BlockSpec(memory_space=pltpu.VMEM)
    hbm = pl.BlockSpec(memory_space=pltpu.HBM)
    return pl.pallas_call(
        functools.partial(kernel, n, m),
        out_shape=pltpu.VMEM((length, out_w), bf16),
        in_specs=[hbm] * 6,
        out_specs=vmem,
        scratch_shapes=[
            pltpu.VMEM((3, length, width), bf16),
            pltpu.VMEM(short_filter.shape, f32),
            pltpu.VMEM(decay_rates.shape, f32),
            pltpu.VMEM(residues.shape, f32),
            pltpu.VMEM((1, width), f32),
            pltpu.VMEM((m, width, out_w), bf16),
            pltpu.VMEM((9 * SUB, LANES), f32),
            table,
            table,
            pltpu.VMEM((SUB, LANES), f32),
            table,
            table,
            table,
            table,
            pltpu.VMEM((3, (length + 2) * SUB, LANES), f32),
            tokens,
            tokens,
            tokens,
            pltpu.VMEM((length, width), bf16),
            pltpu.VMEM((modes * SUB, LANES), bf16),
            pltpu.VMEM((n - 1, modes * SUB, LANES), bf16),
            table,
            pltpu.VMEM((half, length, out_w), bf16),
            pltpu.VMEM((half, length, out_w), bf16),
            pltpu.VMEM((half - 1, length, out_w), bf16),
            pltpu.VMEM((half - 1, length, out_w), bf16),
            pltpu.VMEM((half, length, out_w), f32),
            dma((3, 4)),
            dma((4,)),
            dma((m,)),
            dma((2,)),
            dma((2,)),
            dma((n - 1, 2)),
            dma((n - 1, 2)),
            dma((half, count)),
            dma((half, count)),
            dma((half - 1, count)),
            dma((half - 1, count)),
        ],
        compiler_params=pltpu.CompilerParams(
            collective_id=0, has_side_effects=True, vmem_limit_bytes=60 * 1024 * 1024
        ),
        cost_estimate=pl.CostEstimate(
            flops=2 * length * width * out_w * m, bytes_accessed=2 * width * out_w * m, transcendentals=0
        ),
        name="hyena_layer",
    )(projected, short_filter, decay_rates, residues, skip_gain.reshape(1, width), out_weight)


def solution(mesh):
    in_specs = (
        P(None, ("groups", "ctx"), "chan"),
        P(None, None, "chan"),
        P(None, "chan"),
        P(None, "chan"),
        P("chan"),
        P("chan", None),
    )
    out_specs = P(("groups", "ctx"), "chan")
    return jax.shard_map(body, mesh=mesh, in_specs=in_specs, out_specs=out_specs, check_vma=False)
```

```python
import functools

import jax
import jax.numpy as jnp
from jax import lax
from jax.experimental import pallas as pl
from jax.experimental.pallas import tpu as pltpu
from jax.sharding import PartitionSpec as P

MESH = pl.DeviceIdType.MESH
LANES = 128
SUB = 8
STEP = 16


def parts_of(length):
    return [(0, length // 4), (length // 4, length // 4), (length // 2, length // 2)]


def expm1(v):
    series = jnp.ones_like(v)
    for order in range(9, 1, -1):
        series = 1.0 + series * v * (1.0 / order)
    return jnp.where(v > -0.3, v * series, jnp.exp(v) - 1.0)


def rows(token, count=1):
    start = token * SUB
    if not isinstance(start, int):
        start = pl.multiple_of(start, SUB)
    return pl.ds(start, count * SUB)


def kernel(
    n, m, proj_hbm, sf_hbm, dr_hbm, re_hbm, sg_hbm, w_hbm, out_ref,
    proj, sf_ref, dr_ref, re_ref, sg_ref, wv, sft, dec, res, skip, decay, gain, passing, first_pow,
    sixth, eighth, lead, stored, x, q, g, y, mo, own, arrived, carried, ss, sr, xs, xr, acc,
    proj_sem, small_sem, w_sem, edge_send, edge_recv, state_send, state_recv,
    sib_send, sib_recv, far_send, far_recv,
):
    length, width = proj.shape[1:]
    modes = dr_ref.shape[0]
    blocks = width // LANES
    half = m // 2
    out_w = out_ref.shape[1]
    parts = parts_of(length)
    z, c = lax.axis_index("ctx"), lax.axis_index("chan")
    hi, lo = c // 2, lax.rem(c, 2)
    sibling = hi * 2 + (1 - lo)

    def far(o):
        return lax.rem(hi + o, half) * 2 + lo

    barrier = pltpu.get_barrier_semaphore()
    for off in range(1, n):
        pl.semaphore_signal(barrier, inc=1, device_id={"ctx": lax.rem(z + off, n)}, device_id_type=MESH)
    pl.semaphore_signal(barrier, inc=1, device_id={"chan": sibling}, device_id_type=MESH)
    for o in range(1, half):
        pl.semaphore_signal(barrier, inc=1, device_id={"chan": far(o)}, device_id_type=MESH)

    quarter = length // 4

    def proj_copy(comp, piece):
        token = pl.ds(piece * quarter, quarter)
        return pltpu.make_async_copy(
            proj_hbm.at[comp, token, :], proj.at[comp, token, :], proj_sem.at[comp, piece]
        )

    small = [
        pltpu.make_async_copy(source, target, small_sem.at[index])
        for index, (source, target) in enumerate(
            ((dr_hbm, dr_ref), (re_hbm, re_ref), (sf_hbm, sf_ref), (sg_hbm, sg_ref))
        )
    ]
    for piece in range(4):
        for comp in (1, 2):
            proj_copy(comp, piece).start()
        small[piece].start()
    for piece in range(4):
        proj_copy(0, piece).start()

    def w_copy(o, who):
        target = lax.rem(hi + o, half) * 2 + (lo if who else 1 - lo)
        columns = pl.ds(pl.multiple_of(target * out_w, LANES), out_w)
        slot = 2 * o + who
        return pltpu.make_async_copy(w_hbm.at[:, columns], wv.at[slot], w_sem.at[slot])

    if blocks < SUB:
        for buffer in (sft, dec, res, skip, x):
            buffer[...] = jnp.zeros_like(buffer)

    span = blocks * STEP

    def permutation(height, depth, source):
        row = lax.broadcasted_iota(jnp.int32, (height, depth), 0)
        column = lax.broadcasted_iota(jnp.int32, (height, depth), 1)
        return jnp.where(source(row) == column, 1.0, 0.0).astype(jnp.bfloat16)

    to_token = permutation(STEP * SUB, span, lambda row: (row % SUB) * STEP + row // SUB)
    to_block = permutation(span, STEP * SUB, lambda row: (row % STEP) * SUB + row // STEP)

    def relay(comps, piece):
        for comp in comps:
            proj_copy(comp, piece).wait()
        for t in range(piece * quarter, (piece + 1) * quarter, STEP):
            stacked = [
                jnp.concatenate(
                    [proj[comp, pl.ds(t, STEP), pl.ds(j * LANES, LANES)] for j in range(blocks)], axis=0
                )
                for comp in comps
            ]
            moved = jnp.dot(
                to_token, jnp.concatenate(stacked, axis=1), preferred_element_type=jnp.float32
            )
            for index, comp in enumerate(comps):
                x[comp, rows(t + 2, STEP), :] = moved[:, index * LANES : (index + 1) * LANES]

    for piece in range(4):
        relay((1, 2), piece)

    def edge(index, comp, count):
        return pltpu.make_async_remote_copy(
            src_ref=x.at[pl.ds(comp, count), pl.ds(length * SUB, 2 * SUB), :],
            dst_ref=x.at[pl.ds(comp, count), pl.ds(0, 2 * SUB), :],
            send_sem=edge_send.at[index],
            recv_sem=edge_recv.at[index],
            device_id={"ctx": lax.rem(z + 1, n)},
            device_id_type=MESH,
        )

    pl.semaphore_wait(barrier, (n - 1) + 1 + (half - 1))

    @pl.when(z < n - 1)
    def _():
        edge(0, 1, 2).start()

    for o in list(range(1, half)) + [0]:
        for who in range(2):
            w_copy(o, who).start()

    for copy in small:
        copy.wait()
    for j in range(blocks):
        lanes = pl.ds(j * LANES, LANES)
        dec[pl.ds(j, modes, stride=SUB), :] = dr_ref[:, lanes]
        res[pl.ds(j, modes, stride=SUB), :] = re_ref[:, lanes]
        skip[pl.ds(j, 1), :] = sg_ref[:, lanes]
        for comp in range(3):
            sft[pl.ds(comp * 3 * SUB + j, 3, stride=SUB), :] = sf_ref[comp, :, lanes]
    rate = dec[...]
    decay[...] = jnp.exp(-rate)
    first_pow[...] = jnp.exp(-rate * float(length - 2))
    sixth[...] = jnp.exp(-rate * float(SUB - 2))
    eighth[...] = jnp.exp(-rate * float(SUB))

    def mode(ref, k):
        return ref[pl.ds(k * SUB, SUB), :]

    def short(comp, t, count):
        total = None
        for lag in range(3):
            value = x[comp, rows(t + 2 - lag, count), :].reshape(count, SUB, LANES)
            value = mode(sft, comp * 3 + lag)[None] * value
            total = value if total is None else total + value
        return total

    def mix(t, count):
        gated = (short(1, t, count) * short(2, t, count)).astype(jnp.bfloat16).astype(jnp.float32)
        g[rows(t, count), :] = gated.reshape(count * SUB, LANES)
        return gated

    once = [mode(decay, k) for k in range(modes)]
    twice = [value * value for value in once]

    def horner(state, gated, count):
        for s in range(0, count, 2):
            state = [
                twice[k] * state[k] + (once[k] * gated[s] + gated[s + 1]) for k in range(modes)
            ]
        return state

    state = horner([jnp.zeros((SUB, LANES), jnp.float32)] * modes, mix(2, SUB - 2), SUB - 2)

    def held(i, k):
        return pl.ds(pl.multiple_of((i * modes + k) * SUB, SUB), SUB)

    def own_lap(i, state):
        for k in range(modes):
            stored[held(i, k), :] = state[k]
        return tuple(horner(list(state), mix(i * SUB, SUB), SUB))

    state = list(lax.fori_loop(1, length // SUB, own_lap, tuple(state)))

    @pl.when(z == 0)
    def _():
        x[:, pl.ds(0, 2 * SUB), :] = jnp.zeros((3, 2 * SUB, LANES), jnp.float32)

    @pl.when(z > 0)
    def _():
        edge(0, 1, 2).wait_recv()

    head = mix(0, 2)
    for k in range(0, modes, 2):
        pair = [state[k + e] + mode(first_pow, k + e) * (once[k + e] * head[0] + head[1]) for e in range(2)]
        own[pl.ds(k * SUB, 2 * SUB), :] = jnp.concatenate(pair, axis=0).astype(jnp.bfloat16)

    def send_state(off):
        return pltpu.make_async_remote_copy(
            src_ref=own,
            dst_ref=arrived.at[off - 1],
            send_sem=state_send.at[off - 1],
            recv_sem=state_recv.at[off - 1],
            device_id={"ctx": lax.rem(z + off, n)},
            device_id_type=MESH,
        )

    for off in range(1, n):

        @pl.when(z + off < n)
        def _(off=off):
            send_state(off).start()

    for piece in range(4):
        relay((0,), piece)

    @pl.when(z < n - 1)
    def _():
        edge(1, 0, 1).start()

    gain[...] = res[...] * jnp.sqrt(-expm1(-2.0 * rate))
    passing[...] = jnp.exp(-rate * float(length))
    lead[...] = gain[...] * decay[...]
    power = [mode(gain, k) for k in range(modes)]
    taps = []
    for lag in range(SUB):
        total = skip[...] if lag == 0 else jnp.zeros((SUB, LANES), jnp.float32)
        for k in range(modes):
            total = total + power[k]
            power[k] = power[k] * once[k]
        taps.append(total)

    @pl.loop(0, length // SUB)
    def _(i):
        gated = [g[rows(i * SUB + s), :] for s in range(SUB)]
        for s in range(SUB):
            total = taps[0] * gated[s]
            for lag in range(1, s + 1):
                total = total + taps[lag] * gated[s - lag]
            y[rows(i * SUB + s), :] = total

    @pl.when(z > 0)
    def _():
        edge(1, 0, 1).wait_recv()

    @pl.loop(0, length // STEP)
    def _(i):
        t = i * STEP
        q[rows(t, STEP), :] = short(0, t, STEP).reshape(STEP * SUB, LANES)

    carried[...] = jnp.zeros_like(carried)
    for off in range(n - 1, 0, -1):

        @pl.when(z >= off)
        def _(off=off):
            send_state(off).wait_recv()
            carried[...] = carried[...] * passing[...] + arrived[off - 1].astype(jnp.float32)

    def finish(i, start_state):
        reach = [mode(lead, k) * start_state[k] for k in range(modes)]
        for s in range(SUB):
            token = rows(i * SUB + s)
            sums = [y[token, :], None, None, None]
            for k in range(modes):
                sums[k % 4] = reach[k] if sums[k % 4] is None else sums[k % 4] + reach[k]
                if s < SUB - 1:
                    reach[k] = reach[k] * once[k]
            y[token, :] = q[token, :] * ((sums[0] + sums[1]) + (sums[2] + sums[3]))

    def finish_lap(i, past):
        finish(i, [stored[held(i, k), :] + past[k] for k in range(modes)])
        return tuple(past[k] * mode(eighth, k) for k in range(modes))

    finish(0, [mode(carried, k) for k in range(modes)])
    past = [
        mode(sixth, k) * (twice[k] * mode(carried, k) + (once[k] * head[0] + head[1])) for k in range(modes)
    ]

    def gather(start):
        groups = [
            y[rows(start + e * STEP, STEP), :].astype(jnp.bfloat16) for e in range(quarter // STEP)
        ]
        moved = jnp.dot(
            to_block, jnp.concatenate(groups, axis=1), preferred_element_type=jnp.float32
        ).astype(jnp.bfloat16)
        for e in range(quarter // STEP):
            for j in range(blocks):
                mo[pl.ds(start + e * STEP, STEP), pl.ds(j * LANES, LANES)] = moved[
                    j * STEP : (j + 1) * STEP, e * LANES : (e + 1) * LANES
                ]

    def to_sibling(o, p):
        token = pl.ds(*parts[p]) if o else pl.ds(0, length)
        return pltpu.make_async_remote_copy(
            src_ref=ss.at[o, token, :],
            dst_ref=sr.at[o, token, :],
            send_sem=sib_send.at[o, p],
            recv_sem=sib_recv.at[o, p],
            device_id={"chan": sibling},
            device_id_type=MESH,
        )

    def to_far(o, p):
        token = pl.ds(*parts[p])
        return pltpu.make_async_remote_copy(
            src_ref=xs.at[o - 1, token, :],
            dst_ref=xr.at[o - 1, token, :],
            send_sem=far_send.at[o - 1, p],
            recv_sem=far_recv.at[o - 1, p],
            device_id={"chan": far(o)},
            device_id_type=MESH,
        )

    def product(token, slot):
        return jnp.dot(mo[token, :], wv[slot], preferred_element_type=jnp.float32)

    def forward(p):
        token = pl.ds(*parts[p])
        for o in range(1, half):
            to_sibling(o, p).wait_recv()
            xs[o - 1, token, :] = (acc[o, token, :] + sr[o, token, :].astype(jnp.float32)).astype(jnp.bfloat16)
            to_far(o, p).start()

    for p, (start, count) in enumerate(parts):
        token = pl.ds(start, count)
        past = lax.fori_loop(max(1, start // SUB), (start + count) // SUB, finish_lap, tuple(past))
        for first in range(start, start + count, quarter):
            gather(first)
        if p > 0:
            forward(p - 1)
        for o in range(1, half):
            if p == 0:
                w_copy(o, 0).wait()
            ss[o, token, :] = product(token, 2 * o).astype(jnp.bfloat16)
            to_sibling(o, p).start()
        for o in range(1, half):
            if p == 0:
                w_copy(o, 1).wait()
            acc[o, token, :] = product(token, 2 * o + 1)

    every = pl.ds(0, length)
    w_copy(0, 0).wait()
    ss[0] = product(every, 0).astype(jnp.bfloat16)
    to_sibling(0, 0).start()
    forward(len(parts) - 1)
    w_copy(0, 1).wait()
    acc[0] = product(every, 1)
    to_sibling(0, 0).wait_recv()
    for p, (start, count) in enumerate(parts):
        token = pl.ds(start, count)
        total = acc[0, token, :] + sr[0, token, :].astype(jnp.float32)
        for o in range(1, half):
            to_far(o, p).wait_recv()
            total = total + xr[o - 1, token, :].astype(jnp.float32)
        out_ref[token, :] = total.astype(out_ref.dtype)

    @pl.when(z < n - 1)
    def _():
        edge(0, 1, 2).wait_send()
        edge(1, 0, 1).wait_send()

    for off in range(1, n):

        @pl.when(z + off < n)
        def _(off=off):
            send_state(off).wait_send()

    to_sibling(0, 0).wait_send()
    for p in range(len(parts)):
        for o in range(1, half):
            to_sibling(o, p).wait_send()
            to_far(o, p).wait_send()


def body(projected, short_filter, decay_rates, residues, skip_gain, out_weight):
    n, m = lax.axis_size("ctx"), lax.axis_size("chan")
    length, width = projected.shape[1:]
    modes = decay_rates.shape[0]
    out_w = out_weight.shape[1] // m
    half = m // 2
    count = len(parts_of(length))
    f32, bf16 = jnp.float32, jnp.bfloat16
    table = pltpu.VMEM((modes * SUB, LANES), f32)
    tokens = pltpu.VMEM((length * SUB, LANES), f32)
    dma = pltpu.SemaphoreType.DMA
    vmem = pl.BlockSpec(memory_space=pltpu.VMEM)
    hbm = pl.BlockSpec(memory_space=pltpu.HBM)
    return pl.pallas_call(
        functools.partial(kernel, n, m),
        out_shape=pltpu.VMEM((length, out_w), bf16),
        in_specs=[hbm] * 6,
        out_specs=vmem,
        scratch_shapes=[
            pltpu.VMEM((3, length, width), bf16),
            pltpu.VMEM(short_filter.shape, f32),
            pltpu.VMEM(decay_rates.shape, f32),
            pltpu.VMEM(residues.shape, f32),
            pltpu.VMEM((1, width), f32),
            pltpu.VMEM((m, width, out_w), bf16),
            pltpu.VMEM((9 * SUB, LANES), f32),
            table,
            table,
            pltpu.VMEM((SUB, LANES), f32),
            table,
            table,
            table,
            table,
            table,
            table,
            table,
            pltpu.VMEM((length // SUB * modes * SUB, LANES), f32),
            pltpu.VMEM((3, (length + 2) * SUB, LANES), f32),
            tokens,
            tokens,
            tokens,
            pltpu.VMEM((length, width), bf16),
            pltpu.VMEM((modes * SUB, LANES), bf16),
            pltpu.VMEM((n - 1, modes * SUB, LANES), bf16),
            table,
            pltpu.VMEM((half, length, out_w), bf16),
            pltpu.VMEM((half, length, out_w), bf16),
            pltpu.VMEM((half - 1, length, out_w), bf16),
            pltpu.VMEM((half - 1, length, out_w), bf16),
            pltpu.VMEM((half, length, out_w), f32),
            dma((3, 4)),
            dma((4,)),
            dma((m,)),
            dma((2,)),
            dma((2,)),
            dma((n - 1,)),
            dma((n - 1,)),
            dma((half, count)),
            dma((half, count)),
            dma((half - 1, count)),
            dma((half - 1, count)),
        ],
        compiler_params=pltpu.CompilerParams(
            collective_id=0, has_side_effects=True, vmem_limit_bytes=60 * 1024 * 1024
        ),
        cost_estimate=pl.CostEstimate(
            flops=2 * length * width * out_w * m, bytes_accessed=2 * width * out_w * m, transcendentals=0
        ),
        name="hyena_layer",
    )(projected, short_filter, decay_rates, residues, skip_gain.reshape(1, width), out_weight)


def solution(mesh):
    in_specs = (
        P(None, ("groups", "ctx"), "chan"),
        P(None, None, "chan"),
        P(None, "chan"),
        P(None, "chan"),
        P("chan"),
        P("chan", None),
    )
    out_specs = P(("groups", "ctx"), "chan")
    return jax.shard_map(body, mesh=mesh, in_specs=in_specs, out_specs=out_specs, check_vma=False)
```

```python
import functools

import jax
import jax.numpy as jnp
from jax import lax
from jax.experimental import pallas as pl
from jax.experimental.pallas import tpu as pltpu
from jax.sharding import PartitionSpec as P

MESH = pl.DeviceIdType.MESH
LANES = 128
SUB = 8
STEP = 16


def parts_of(length):
    return [(0, length // 4), (length // 4, length // 4), (length // 2, length // 2)]


def expm1(v):
    series = jnp.ones_like(v)
    for order in range(9, 1, -1):
        series = 1.0 + series * v * (1.0 / order)
    return jnp.where(v > -0.3, v * series, jnp.exp(v) - 1.0)


def rows(token, count=1):
    start = token * SUB
    if not isinstance(start, int):
        start = pl.multiple_of(start, SUB)
    return pl.ds(start, count * SUB)


def kernel(
    n, m, proj_hbm, sf_hbm, dr_hbm, re_hbm, sg_hbm, w_hbm, out_ref,
    proj, sf_ref, dr_ref, re_ref, sg_ref, wv, sft, dec, res, skip, decay, gain, passing, first_pow,
    sixth, eighth, lead, stored, x, q, g, y, mo, own, arrived, carried, ss, sr, xs, xr, acc,
    proj_sem, small_sem, w_sem, edge_send, edge_recv, state_send, state_recv,
    sib_send, sib_recv, far_send, far_recv,
):
    length, width = proj.shape[1:]
    modes = dr_ref.shape[0]
    blocks = width // LANES
    half = m // 2
    out_w = out_ref.shape[1]
    parts = parts_of(length)
    z, c = lax.axis_index("ctx"), lax.axis_index("chan")
    hi, lo = c // 2, lax.rem(c, 2)
    sibling = hi * 2 + (1 - lo)

    def far(o):
        return lax.rem(hi + o, half) * 2 + lo

    barrier = pltpu.get_barrier_semaphore()
    for off in range(1, n):
        pl.semaphore_signal(barrier, inc=1, device_id={"ctx": lax.rem(z + off, n)}, device_id_type=MESH)
    pl.semaphore_signal(barrier, inc=1, device_id={"chan": sibling}, device_id_type=MESH)
    for o in range(1, half):
        pl.semaphore_signal(barrier, inc=1, device_id={"chan": far(o)}, device_id_type=MESH)

    quarter = length // 4

    def proj_copy(comp, piece):
        token = pl.ds(piece * quarter, quarter)
        return pltpu.make_async_copy(
            proj_hbm.at[comp, token, :], proj.at[comp, token, :], proj_sem.at[comp, piece]
        )

    small = [
        pltpu.make_async_copy(source, target, small_sem.at[index])
        for index, (source, target) in enumerate(
            ((dr_hbm, dr_ref), (re_hbm, re_ref), (sf_hbm, sf_ref), (sg_hbm, sg_ref))
        )
    ]
    for index, piece in enumerate((3, 0, 1, 2)):
        for comp in (1, 2):
            proj_copy(comp, piece).start()
        small[index].start()
    for piece in range(4):
        proj_copy(0, piece).start()

    def w_copy(o, who):
        target = lax.rem(hi + o, half) * 2 + (lo if who else 1 - lo)
        columns = pl.ds(pl.multiple_of(target * out_w, LANES), out_w)
        slot = 2 * o + who
        return pltpu.make_async_copy(w_hbm.at[:, columns], wv.at[slot], w_sem.at[slot])

    if blocks < SUB:
        for buffer in (sft, dec, res, skip, x):
            buffer[...] = jnp.zeros_like(buffer)

    span = blocks * STEP

    def permutation(height, depth, source):
        row = lax.broadcasted_iota(jnp.int32, (height, depth), 0)
        column = lax.broadcasted_iota(jnp.int32, (height, depth), 1)
        return jnp.where(source(row) == column, 1.0, 0.0).astype(jnp.bfloat16)

    to_token = permutation(STEP * SUB, span, lambda row: (row % SUB) * STEP + row // SUB)
    to_block = permutation(span, STEP * SUB, lambda row: (row % STEP) * SUB + row // STEP)

    def relay(comps, piece):
        for comp in comps:
            proj_copy(comp, piece).wait()
        for t in range(piece * quarter, (piece + 1) * quarter, STEP):
            stacked = [
                jnp.concatenate(
                    [proj[comp, pl.ds(t, STEP), pl.ds(j * LANES, LANES)] for j in range(blocks)], axis=0
                )
                for comp in comps
            ]
            moved = jnp.dot(
                to_token, jnp.concatenate(stacked, axis=1), preferred_element_type=jnp.float32
            )
            for index, comp in enumerate(comps):
                x[comp, rows(t + 2, STEP), :] = moved[:, index * LANES : (index + 1) * LANES]

    relay((1, 2), 3)

    def edge(index, comp, count):
        return pltpu.make_async_remote_copy(
            src_ref=x.at[pl.ds(comp, count), pl.ds(length * SUB, 2 * SUB), :],
            dst_ref=x.at[pl.ds(comp, count), pl.ds(0, 2 * SUB), :],
            send_sem=edge_send.at[index],
            recv_sem=edge_recv.at[index],
            device_id={"ctx": lax.rem(z + 1, n)},
            device_id_type=MESH,
        )

    pl.semaphore_wait(barrier, (n - 1) + 1 + (half - 1))

    @pl.when(z < n - 1)
    def _():
        edge(0, 1, 2).start()

    for piece in range(3):
        relay((1, 2), piece)

    for o in list(range(1, half)) + [0]:
        for who in range(2):
            w_copy(o, who).start()

    for copy in small:
        copy.wait()
    for j in range(blocks):
        lanes = pl.ds(j * LANES, LANES)
        dec[pl.ds(j, modes, stride=SUB), :] = dr_ref[:, lanes]
        res[pl.ds(j, modes, stride=SUB), :] = re_ref[:, lanes]
        skip[pl.ds(j, 1), :] = sg_ref[:, lanes]
        for comp in range(3):
            sft[pl.ds(comp * 3 * SUB + j, 3, stride=SUB), :] = sf_ref[comp, :, lanes]
    rate = dec[...]
    decay[...] = jnp.exp(-rate)
    first_pow[...] = jnp.exp(-rate * float(length - 2))
    sixth[...] = jnp.exp(-rate * float(SUB - 2))
    eighth[...] = jnp.exp(-rate * float(SUB))

    def mode(ref, k):
        return ref[pl.ds(k * SUB, SUB), :]

    def short(comp, t, count):
        total = None
        for lag in range(3):
            value = x[comp, rows(t + 2 - lag, count), :].reshape(count, SUB, LANES)
            value = mode(sft, comp * 3 + lag)[None] * value
            total = value if total is None else total + value
        return total

    def mix(t, count):
        gated = (short(1, t, count) * short(2, t, count)).astype(jnp.bfloat16).astype(jnp.float32)
        g[rows(t, count), :] = gated.reshape(count * SUB, LANES)
        return gated

    once = [mode(decay, k) for k in range(modes)]
    twice = [value * value for value in once]

    def horner(group, state, gated, count):
        for s in range(0, count, 2):
            state = [
                twice[k] * value + (once[k] * gated[s] + gated[s + 1]) for k, value in zip(group, state)
            ]
        return state

    def held(i, k):
        return pl.ds(pl.multiple_of((i * modes + k) * SUB, SUB), SUB)

    zero = jnp.zeros((SUB, LANES), jnp.float32)
    groups = [range(0, modes // 2), range(modes // 2, modes)]

    def own_lap(group, gated_of, i, state):
        for k, value in zip(group, state):
            stored[held(i, k), :] = value
        return tuple(horner(group, list(state), gated_of(i * SUB, SUB), SUB))

    def own_pass(group, gated_of):
        state = horner(group, [zero] * len(group), gated_of(2, SUB - 2), SUB - 2)
        lap = functools.partial(own_lap, group, gated_of)
        return lax.fori_loop(1, length // SUB, lap, tuple(state))

    state = own_pass(groups[0], mix)

    @pl.when(z == 0)
    def _():
        x[:, pl.ds(0, 2 * SUB), :] = jnp.zeros((3, 2 * SUB, LANES), jnp.float32)

    @pl.when(z > 0)
    def _():
        edge(0, 1, 2).wait_recv()

    head = mix(0, 2)

    def send_state(off, part):
        piece = pl.ds(groups[part][0] * SUB, len(groups[part]) * SUB)
        return pltpu.make_async_remote_copy(
            src_ref=own.at[piece, :],
            dst_ref=arrived.at[off - 1, piece, :],
            send_sem=state_send.at[off - 1, part],
            recv_sem=state_recv.at[off - 1, part],
            device_id={"ctx": lax.rem(z + off, n)},
            device_id_type=MESH,
        )

    def publish(part, state):
        group = groups[part]
        whole = [
            value + mode(first_pow, k) * (once[k] * head[0] + head[1]) for k, value in zip(group, state)
        ]
        for index in range(0, len(group), 2):
            pair = jnp.concatenate(whole[index : index + 2], axis=0)
            own[pl.ds(group[index] * SUB, 2 * SUB), :] = pair.astype(jnp.bfloat16)
        for off in range(1, n):

            @pl.when(z + off < n)
            def _(off=off):
                send_state(off, part).start()

    def mixed_before(t, count):
        return g[rows(t, count), :].reshape(count, SUB, LANES)

    publish(0, state)
    publish(1, own_pass(groups[1], mixed_before))

    for piece in range(4):
        relay((0,), piece)

    @pl.when(z < n - 1)
    def _():
        edge(1, 0, 1).start()

    gain[...] = res[...] * jnp.sqrt(-expm1(-2.0 * rate))
    passing[...] = jnp.exp(-rate * float(length))
    lead[...] = gain[...] * decay[...]
    power = [mode(gain, k) for k in range(modes)]
    taps = []
    for lag in range(SUB):
        total = skip[...] if lag == 0 else jnp.zeros((SUB, LANES), jnp.float32)
        for k in range(modes):
            total = total + power[k]
            power[k] = power[k] * once[k]
        taps.append(total)

    @pl.loop(0, length // SUB)
    def _(i):
        gated = [g[rows(i * SUB + s), :] for s in range(SUB)]
        for s in range(SUB):
            total = taps[0] * gated[s]
            for lag in range(1, s + 1):
                total = total + taps[lag] * gated[s - lag]
            y[rows(i * SUB + s), :] = total

    @pl.when(z > 0)
    def _():
        edge(1, 0, 1).wait_recv()

    @pl.loop(0, length // STEP)
    def _(i):
        t = i * STEP
        q[rows(t, STEP), :] = short(0, t, STEP).reshape(STEP * SUB, LANES)

    carried[...] = jnp.zeros_like(carried)
    for off in range(n - 1, 0, -1):

        @pl.when(z >= off)
        def _(off=off):
            for part in range(2):
                send_state(off, part).wait_recv()
            carried[...] = carried[...] * passing[...] + arrived[off - 1].astype(jnp.float32)

    def finish(i, start_state):
        reach = [mode(lead, k) * start_state[k] for k in range(modes)]
        for s in range(SUB):
            token = rows(i * SUB + s)
            sums = [y[token, :], None, None, None]
            for k in range(modes):
                sums[k % 4] = reach[k] if sums[k % 4] is None else sums[k % 4] + reach[k]
                if s < SUB - 1:
                    reach[k] = reach[k] * once[k]
            y[token, :] = q[token, :] * ((sums[0] + sums[1]) + (sums[2] + sums[3]))

    def finish_lap(i, past):
        finish(i, [stored[held(i, k), :] + past[k] for k in range(modes)])
        return tuple(past[k] * mode(eighth, k) for k in range(modes))

    finish(0, [mode(carried, k) for k in range(modes)])
    past = [
        mode(sixth, k) * (twice[k] * mode(carried, k) + (once[k] * head[0] + head[1])) for k in range(modes)
    ]

    def gather(start):
        columns = [
            y[rows(start + e * STEP, STEP), :].astype(jnp.bfloat16) for e in range(quarter // STEP)
        ]
        moved = jnp.dot(
            to_block, jnp.concatenate(columns, axis=1), preferred_element_type=jnp.float32
        ).astype(jnp.bfloat16)
        for e in range(quarter // STEP):
            for j in range(blocks):
                mo[pl.ds(start + e * STEP, STEP), pl.ds(j * LANES, LANES)] = moved[
                    j * STEP : (j + 1) * STEP, e * LANES : (e + 1) * LANES
                ]

    def to_sibling(o, p):
        token = pl.ds(*parts[p]) if o else pl.ds(0, length)
        return pltpu.make_async_remote_copy(
            src_ref=ss.at[o, token, :],
            dst_ref=sr.at[o, token, :],
            send_sem=sib_send.at[o, p],
            recv_sem=sib_recv.at[o, p],
            device_id={"chan": sibling},
            device_id_type=MESH,
        )

    def to_far(o, p):
        token = pl.ds(*parts[p])
        return pltpu.make_async_remote_copy(
            src_ref=xs.at[o - 1, token, :],
            dst_ref=xr.at[o - 1, token, :],
            send_sem=far_send.at[o - 1, p],
            recv_sem=far_recv.at[o - 1, p],
            device_id={"chan": far(o)},
            device_id_type=MESH,
        )

    def product(token, slot):
        return jnp.dot(mo[token, :], wv[slot], preferred_element_type=jnp.float32)

    def forward(p):
        token = pl.ds(*parts[p])
        for o in range(1, half):
            to_sibling(o, p).wait_recv()
            xs[o - 1, token, :] = (acc[o, token, :] + sr[o, token, :].astype(jnp.float32)).astype(jnp.bfloat16)
            to_far(o, p).start()

    for p, (start, count) in enumerate(parts):
        token = pl.ds(start, count)
        past = lax.fori_loop(max(1, start // SUB), (start + count) // SUB, finish_lap, tuple(past))
        for first in range(start, start + count, quarter):
            gather(first)
        if p > 0:
            forward(p - 1)
        for o in range(1, half):
            if p == 0:
                w_copy(o, 0).wait()
            ss[o, token, :] = product(token, 2 * o).astype(jnp.bfloat16)
            to_sibling(o, p).start()
        for o in range(1, half):
            if p == 0:
                w_copy(o, 1).wait()
            acc[o, token, :] = product(token, 2 * o + 1)

    every = pl.ds(0, length)
    w_copy(0, 0).wait()
    ss[0] = product(every, 0).astype(jnp.bfloat16)
    to_sibling(0, 0).start()
    forward(len(parts) - 1)
    w_copy(0, 1).wait()
    acc[0] = product(every, 1)
    to_sibling(0, 0).wait_recv()
    for p, (start, count) in enumerate(parts):
        token = pl.ds(start, count)
        total = acc[0, token, :] + sr[0, token, :].astype(jnp.float32)
        for o in range(1, half):
            to_far(o, p).wait_recv()
            total = total + xr[o - 1, token, :].astype(jnp.float32)
        out_ref[token, :] = total.astype(out_ref.dtype)

    @pl.when(z < n - 1)
    def _():
        edge(0, 1, 2).wait_send()
        edge(1, 0, 1).wait_send()

    for off in range(1, n):

        @pl.when(z + off < n)
        def _(off=off):
            for part in range(2):
                send_state(off, part).wait_send()

    to_sibling(0, 0).wait_send()
    for p in range(len(parts)):
        for o in range(1, half):
            to_sibling(o, p).wait_send()
            to_far(o, p).wait_send()


def body(projected, short_filter, decay_rates, residues, skip_gain, out_weight):
    n, m = lax.axis_size("ctx"), lax.axis_size("chan")
    length, width = projected.shape[1:]
    modes = decay_rates.shape[0]
    out_w = out_weight.shape[1] // m
    half = m // 2
    count = len(parts_of(length))
    f32, bf16 = jnp.float32, jnp.bfloat16
    table = pltpu.VMEM((modes * SUB, LANES), f32)
    tokens = pltpu.VMEM((length * SUB, LANES), f32)
    dma = pltpu.SemaphoreType.DMA
    vmem = pl.BlockSpec(memory_space=pltpu.VMEM)
    hbm = pl.BlockSpec(memory_space=pltpu.HBM)
    return pl.pallas_call(
        functools.partial(kernel, n, m),
        out_shape=pltpu.VMEM((length, out_w), bf16),
        in_specs=[hbm] * 6,
        out_specs=vmem,
        scratch_shapes=[
            pltpu.VMEM((3, length, width), bf16),
            pltpu.VMEM(short_filter.shape, f32),
            pltpu.VMEM(decay_rates.shape, f32),
            pltpu.VMEM(residues.shape, f32),
            pltpu.VMEM((1, width), f32),
            pltpu.VMEM((m, width, out_w), bf16),
            pltpu.VMEM((9 * SUB, LANES), f32),
            table,
            table,
            pltpu.VMEM((SUB, LANES), f32),
            table,
            table,
            table,
            table,
            table,
            table,
            table,
            pltpu.VMEM((length // SUB * modes * SUB, LANES), f32),
            pltpu.VMEM((3, (length + 2) * SUB, LANES), f32),
            tokens,
            tokens,
            tokens,
            pltpu.VMEM((length, width), bf16),
            pltpu.VMEM((modes * SUB, LANES), bf16),
            pltpu.VMEM((n - 1, modes * SUB, LANES), bf16),
            table,
            pltpu.VMEM((half, length, out_w), bf16),
            pltpu.VMEM((half, length, out_w), bf16),
            pltpu.VMEM((half - 1, length, out_w), bf16),
            pltpu.VMEM((half - 1, length, out_w), bf16),
            pltpu.VMEM((half, length, out_w), f32),
            dma((3, 4)),
            dma((4,)),
            dma((m,)),
            dma((2,)),
            dma((2,)),
            dma((n - 1, 2)),
            dma((n - 1, 2)),
            dma((half, count)),
            dma((half, count)),
            dma((half - 1, count)),
            dma((half - 1, count)),
        ],
        compiler_params=pltpu.CompilerParams(
            collective_id=0, has_side_effects=True, vmem_limit_bytes=60 * 1024 * 1024
        ),
        cost_estimate=pl.CostEstimate(
            flops=2 * length * width * out_w * m, bytes_accessed=2 * width * out_w * m, transcendentals=0
        ),
        name="hyena_layer",
    )(projected, short_filter, decay_rates, residues, skip_gain.reshape(1, width), out_weight)


def solution(mesh):
    in_specs = (
        P(None, ("groups", "ctx"), "chan"),
        P(None, None, "chan"),
        P(None, "chan"),
        P(None, "chan"),
        P("chan"),
        P("chan", None),
    )
    out_specs = P(("groups", "ctx"), "chan")
    return jax.shard_map(body, mesh=mesh, in_specs=in_specs, out_specs=out_specs, check_vma=False)
```

```python
import functools

import jax
import jax.numpy as jnp
from jax import lax
from jax.experimental import pallas as pl
from jax.experimental.pallas import tpu as pltpu
from jax.sharding import PartitionSpec as P

MESH = pl.DeviceIdType.MESH
LANES = 128
SUB = 8
STEP = 16


def parts_of(length):
    return [(0, length // 4), (length // 4, length // 4), (length // 2, length // 2)]


def expm1(v):
    series = jnp.ones_like(v)
    for order in range(9, 1, -1):
        series = 1.0 + series * v * (1.0 / order)
    return jnp.where(v > -0.3, v * series, jnp.exp(v) - 1.0)


def rows(token, count=1):
    start = token * SUB
    if not isinstance(start, int):
        start = pl.multiple_of(start, SUB)
    return pl.ds(start, count * SUB)


def kernel(
    n, m, proj_hbm, sf_hbm, dr_hbm, re_hbm, sg_hbm, w_hbm, out_ref,
    proj, sf_ref, dr_ref, re_ref, sg_ref, wv, sft, dec, res, skip, decay, gain, passing, first_pow,
    sixth, eighth, lead, stored, x, q, g, y, mo, own, arrived, carried, ss, sr, xs, xr, acc,
    proj_sem, small_sem, w_sem, edge_send, edge_recv, state_send, state_recv,
    sib_send, sib_recv, far_send, far_recv,
):
    length, width = proj.shape[1:]
    modes = dr_ref.shape[0]
    blocks = width // LANES
    half = m // 2
    out_w = out_ref.shape[1]
    parts = parts_of(length)
    z, c = lax.axis_index("ctx"), lax.axis_index("chan")
    hi, lo = c // 2, lax.rem(c, 2)
    sibling = hi * 2 + (1 - lo)

    def far(o):
        return lax.rem(hi + o, half) * 2 + lo

    barrier = pltpu.get_barrier_semaphore()
    for off in range(1, n):
        pl.semaphore_signal(barrier, inc=1, device_id={"ctx": lax.rem(z + off, n)}, device_id_type=MESH)
    pl.semaphore_signal(barrier, inc=1, device_id={"chan": sibling}, device_id_type=MESH)
    for o in range(1, half):
        pl.semaphore_signal(barrier, inc=1, device_id={"chan": far(o)}, device_id_type=MESH)

    quarter = length // 4

    def proj_copy(comp, piece):
        token = pl.ds(piece * quarter, quarter)
        return pltpu.make_async_copy(
            proj_hbm.at[comp, token, :], proj.at[comp, token, :], proj_sem.at[comp, piece]
        )

    small = [
        pltpu.make_async_copy(source, target, small_sem.at[index])
        for index, (source, target) in enumerate(
            ((dr_hbm, dr_ref), (re_hbm, re_ref), (sf_hbm, sf_ref), (sg_hbm, sg_ref))
        )
    ]
    for piece in range(4):
        for comp in (1, 2):
            proj_copy(comp, piece).start()
        small[piece].start()
    for piece in range(4):
        proj_copy(0, piece).start()

    def w_copy(o, who):
        target = lax.rem(hi + o, half) * 2 + (lo if who else 1 - lo)
        columns = pl.ds(pl.multiple_of(target * out_w, LANES), out_w)
        slot = 2 * o + who
        return pltpu.make_async_copy(w_hbm.at[:, columns], wv.at[slot], w_sem.at[slot])

    if blocks < SUB:
        for buffer in (sft, dec, res, skip, x):
            buffer[...] = jnp.zeros_like(buffer)

    span = blocks * STEP

    def permutation(height, depth, source):
        row = lax.broadcasted_iota(jnp.int32, (height, depth), 0)
        column = lax.broadcasted_iota(jnp.int32, (height, depth), 1)
        return jnp.where(source(row) == column, 1.0, 0.0).astype(jnp.bfloat16)

    to_token = permutation(STEP * SUB, span, lambda row: (row % SUB) * STEP + row // SUB)
    to_block = permutation(span, STEP * SUB, lambda row: (row % STEP) * SUB + row // STEP)

    def relay(comps, piece):
        for comp in comps:
            proj_copy(comp, piece).wait()
        for t in range(piece * quarter, (piece + 1) * quarter, STEP):
            stacked = [
                jnp.concatenate(
                    [proj[comp, pl.ds(t, STEP), pl.ds(j * LANES, LANES)] for j in range(blocks)], axis=0
                )
                for comp in comps
            ]
            moved = jnp.dot(
                to_token, jnp.concatenate(stacked, axis=1), preferred_element_type=jnp.float32
            )
            for index, comp in enumerate(comps):
                x[comp, rows(t + 2, STEP), :] = moved[:, index * LANES : (index + 1) * LANES]

    for piece in range(4):
        relay((1, 2), piece)

    def edge(index, comp, count):
        return pltpu.make_async_remote_copy(
            src_ref=x.at[pl.ds(comp, count), pl.ds(length * SUB, 2 * SUB), :],
            dst_ref=x.at[pl.ds(comp, count), pl.ds(0, 2 * SUB), :],
            send_sem=edge_send.at[index],
            recv_sem=edge_recv.at[index],
            device_id={"ctx": lax.rem(z + 1, n)},
            device_id_type=MESH,
        )

    pl.semaphore_wait(barrier, (n - 1) + 1 + (half - 1))

    @pl.when(z < n - 1)
    def _():
        edge(0, 1, 2).start()

    for o in list(range(1, half)) + [0]:
        for who in range(2):
            w_copy(o, who).start()

    for copy in small:
        copy.wait()
    for j in range(blocks):
        lanes = pl.ds(j * LANES, LANES)
        dec[pl.ds(j, modes, stride=SUB), :] = dr_ref[:, lanes]
        res[pl.ds(j, modes, stride=SUB), :] = re_ref[:, lanes]
        skip[pl.ds(j, 1), :] = sg_ref[:, lanes]
        for comp in range(3):
            sft[pl.ds(comp * 3 * SUB + j, 3, stride=SUB), :] = sf_ref[comp, :, lanes]
    rate = dec[...]
    decay[...] = jnp.exp(-rate)
    first_pow[...] = jnp.exp(-rate * float(length - 2))
    sixth[...] = jnp.exp(-rate * float(SUB - 2))
    eighth[...] = jnp.exp(-rate * float(SUB))

    def mode(ref, k):
        return ref[pl.ds(k * SUB, SUB), :]

    def short(comp, t, count):
        total = None
        for lag in range(3):
            value = x[comp, rows(t + 2 - lag, count), :].reshape(count, SUB, LANES)
            value = mode(sft, comp * 3 + lag)[None] * value
            total = value if total is None else total + value
        return total

    def mix(t, count):
        gated = (short(1, t, count) * short(2, t, count)).astype(jnp.bfloat16).astype(jnp.float32)
        g[rows(t, count), :] = gated.reshape(count * SUB, LANES)
        return gated

    once = [mode(decay, k) for k in range(modes)]
    twice = [value * value for value in once]

    def horner(state, gated, count):
        for s in range(0, count, 2):
            state = [
                twice[k] * state[k] + (once[k] * gated[s] + gated[s + 1]) for k in range(modes)
            ]
        return state

    state = horner([jnp.zeros((SUB, LANES), jnp.float32)] * modes, mix(2, SUB - 2), SUB - 2)

    def held(i, k):
        return rows(i * modes + k)

    def own_lap(i, state):
        for k in range(modes):
            stored[held(i, k), :] = state[k]
        return tuple(horner(list(state), mix(i * SUB, SUB), SUB))

    def paired(lap):
        return lambda i, carry: lap(2 * i + 1, lap(2 * i, carry))

    state = own_lap(1, state)
    state = list(lax.fori_loop(1, length // SUB // 2, paired(own_lap), tuple(state)))

    @pl.when(z == 0)
    def _():
        x[:, pl.ds(0, 2 * SUB), :] = jnp.zeros((3, 2 * SUB, LANES), jnp.float32)

    @pl.when(z > 0)
    def _():
        edge(0, 1, 2).wait_recv()

    head = mix(0, 2)
    for k in range(0, modes, 2):
        pair = [state[k + e] + mode(first_pow, k + e) * (once[k + e] * head[0] + head[1]) for e in range(2)]
        own[pl.ds(k * SUB, 2 * SUB), :] = jnp.concatenate(pair, axis=0).astype(jnp.bfloat16)

    def send_state(off):
        return pltpu.make_async_remote_copy(
            src_ref=own,
            dst_ref=arrived.at[off - 1],
            send_sem=state_send.at[off - 1],
            recv_sem=state_recv.at[off - 1],
            device_id={"ctx": lax.rem(z + off, n)},
            device_id_type=MESH,
        )

    for off in range(1, n):

        @pl.when(z + off < n)
        def _(off=off):
            send_state(off).start()

    for piece in range(4):
        relay((0,), piece)

    @pl.when(z < n - 1)
    def _():
        edge(1, 0, 1).start()

    gain[...] = res[...] * jnp.sqrt(-expm1(-2.0 * rate))
    passing[...] = jnp.exp(-rate * float(length))
    lead[...] = gain[...] * decay[...]
    power = [mode(gain, k) for k in range(modes)]
    taps = []
    for lag in range(SUB):
        total = skip[...] if lag == 0 else jnp.zeros((SUB, LANES), jnp.float32)
        for k in range(modes):
            total = total + power[k]
            power[k] = power[k] * once[k]
        taps.append(total)

    @pl.loop(0, length // SUB)
    def _(i):
        gated = [g[rows(i * SUB + s), :] for s in range(SUB)]
        for s in range(SUB):
            total = taps[0] * gated[s]
            for lag in range(1, s + 1):
                total = total + taps[lag] * gated[s - lag]
            y[rows(i * SUB + s), :] = total

    @pl.when(z > 0)
    def _():
        edge(1, 0, 1).wait_recv()

    @pl.loop(0, length // STEP)
    def _(i):
        t = i * STEP
        q[rows(t, STEP), :] = short(0, t, STEP).reshape(STEP * SUB, LANES)

    carried[...] = jnp.zeros_like(carried)
    for off in range(n - 1, 0, -1):

        @pl.when(z >= off)
        def _(off=off):
            send_state(off).wait_recv()
            carried[...] = carried[...] * passing[...] + arrived[off - 1].astype(jnp.float32)

    def finish(i, start_state):
        reach = [mode(lead, k) * start_state[k] for k in range(modes)]
        for s in range(SUB):
            token = rows(i * SUB + s)
            sums = [y[token, :], None, None, None]
            for k in range(modes):
                sums[k % 4] = reach[k] if sums[k % 4] is None else sums[k % 4] + reach[k]
                if s < SUB - 1:
                    reach[k] = reach[k] * once[k]
            y[token, :] = q[token, :] * ((sums[0] + sums[1]) + (sums[2] + sums[3]))

    def finish_lap(i, past):
        finish(i, [stored[held(i, k), :] + past[k] for k in range(modes)])
        return tuple(past[k] * mode(eighth, k) for k in range(modes))

    finish(0, [mode(carried, k) for k in range(modes)])
    past = [
        mode(sixth, k) * (twice[k] * mode(carried, k) + (once[k] * head[0] + head[1])) for k in range(modes)
    ]

    def gather(start):
        groups = [
            y[rows(start + e * STEP, STEP), :].astype(jnp.bfloat16) for e in range(quarter // STEP)
        ]
        moved = jnp.dot(
            to_block, jnp.concatenate(groups, axis=1), preferred_element_type=jnp.float32
        ).astype(jnp.bfloat16)
        for e in range(quarter // STEP):
            for j in range(blocks):
                mo[pl.ds(start + e * STEP, STEP), pl.ds(j * LANES, LANES)] = moved[
                    j * STEP : (j + 1) * STEP, e * LANES : (e + 1) * LANES
                ]

    def to_sibling(o, p):
        token = pl.ds(*parts[p]) if o else pl.ds(0, length)
        return pltpu.make_async_remote_copy(
            src_ref=ss.at[o, token, :],
            dst_ref=sr.at[o, token, :],
            send_sem=sib_send.at[o, p],
            recv_sem=sib_recv.at[o, p],
            device_id={"chan": sibling},
            device_id_type=MESH,
        )

    def to_far(o, p):
        token = pl.ds(*parts[p])
        return pltpu.make_async_remote_copy(
            src_ref=xs.at[o - 1, token, :],
            dst_ref=xr.at[o - 1, token, :],
            send_sem=far_send.at[o - 1, p],
            recv_sem=far_recv.at[o - 1, p],
            device_id={"chan": far(o)},
            device_id_type=MESH,
        )

    def product(token, slot):
        return jnp.dot(mo[token, :], wv[slot], preferred_element_type=jnp.float32)

    def forward(p):
        token = pl.ds(*parts[p])
        for o in range(1, half):
            to_sibling(o, p).wait_recv()
            xs[o - 1, token, :] = (acc[o, token, :] + sr[o, token, :].astype(jnp.float32)).astype(jnp.bfloat16)
            to_far(o, p).start()

    for p, (start, count) in enumerate(parts):
        token = pl.ds(start, count)
        if p == 0:
            past = finish_lap(1, past)
        first, last = max(1, start // SUB // 2), (start + count) // SUB // 2
        past = lax.fori_loop(first, last, paired(finish_lap), tuple(past))
        for first in range(start, start + count, quarter):
            gather(first)
        if p > 0:
            forward(p - 1)
        for o in range(1, half):
            if p == 0:
                w_copy(o, 0).wait()
            ss[o, token, :] = product(token, 2 * o).astype(jnp.bfloat16)
            to_sibling(o, p).start()
        for o in range(1, half):
            if p == 0:
                w_copy(o, 1).wait()
            acc[o, token, :] = product(token, 2 * o + 1)

    every = pl.ds(0, length)
    w_copy(0, 0).wait()
    ss[0] = product(every, 0).astype(jnp.bfloat16)
    to_sibling(0, 0).start()
    forward(len(parts) - 1)
    w_copy(0, 1).wait()
    acc[0] = product(every, 1)
    to_sibling(0, 0).wait_recv()
    for p, (start, count) in enumerate(parts):
        token = pl.ds(start, count)
        total = acc[0, token, :] + sr[0, token, :].astype(jnp.float32)
        for o in range(1, half):
            to_far(o, p).wait_recv()
            total = total + xr[o - 1, token, :].astype(jnp.float32)
        out_ref[token, :] = total.astype(out_ref.dtype)

    @pl.when(z < n - 1)
    def _():
        edge(0, 1, 2).wait_send()
        edge(1, 0, 1).wait_send()

    for off in range(1, n):

        @pl.when(z + off < n)
        def _(off=off):
            send_state(off).wait_send()

    to_sibling(0, 0).wait_send()
    for p in range(len(parts)):
        for o in range(1, half):
            to_sibling(o, p).wait_send()
            to_far(o, p).wait_send()


def body(projected, short_filter, decay_rates, residues, skip_gain, out_weight):
    n, m = lax.axis_size("ctx"), lax.axis_size("chan")
    length, width = projected.shape[1:]
    modes = decay_rates.shape[0]
    out_w = out_weight.shape[1] // m
    half = m // 2
    count = len(parts_of(length))
    f32, bf16 = jnp.float32, jnp.bfloat16
    table = pltpu.VMEM((modes * SUB, LANES), f32)
    tokens = pltpu.VMEM((length * SUB, LANES), f32)
    dma = pltpu.SemaphoreType.DMA
    vmem = pl.BlockSpec(memory_space=pltpu.VMEM)
    hbm = pl.BlockSpec(memory_space=pltpu.HBM)
    return pl.pallas_call(
        functools.partial(kernel, n, m),
        out_shape=pltpu.VMEM((length, out_w), bf16),
        in_specs=[hbm] * 6,
        out_specs=vmem,
        scratch_shapes=[
            pltpu.VMEM((3, length, width), bf16),
            pltpu.VMEM(short_filter.shape, f32),
            pltpu.VMEM(decay_rates.shape, f32),
            pltpu.VMEM(residues.shape, f32),
            pltpu.VMEM((1, width), f32),
            pltpu.VMEM((m, width, out_w), bf16),
            pltpu.VMEM((9 * SUB, LANES), f32),
            table,
            table,
            pltpu.VMEM((SUB, LANES), f32),
            table,
            table,
            table,
            table,
            table,
            table,
            table,
            pltpu.VMEM((length // SUB * modes * SUB, LANES), f32),
            pltpu.VMEM((3, (length + 2) * SUB, LANES), f32),
            tokens,
            tokens,
            tokens,
            pltpu.VMEM((length, width), bf16),
            pltpu.VMEM((modes * SUB, LANES), bf16),
            pltpu.VMEM((n - 1, modes * SUB, LANES), bf16),
            table,
            pltpu.VMEM((half, length, out_w), bf16),
            pltpu.VMEM((half, length, out_w), bf16),
            pltpu.VMEM((half - 1, length, out_w), bf16),
            pltpu.VMEM((half - 1, length, out_w), bf16),
            pltpu.VMEM((half, length, out_w), f32),
            dma((3, 4)),
            dma((4,)),
            dma((m,)),
            dma((2,)),
            dma((2,)),
            dma((n - 1,)),
            dma((n - 1,)),
            dma((half, count)),
            dma((half, count)),
            dma((half - 1, count)),
            dma((half - 1, count)),
        ],
        compiler_params=pltpu.CompilerParams(
            collective_id=0, has_side_effects=True, vmem_limit_bytes=60 * 1024 * 1024
        ),
        cost_estimate=pl.CostEstimate(
            flops=2 * length * width * out_w * m, bytes_accessed=2 * width * out_w * m, transcendentals=0
        ),
        name="hyena_layer",
    )(projected, short_filter, decay_rates, residues, skip_gain.reshape(1, width), out_weight)


def solution(mesh):
    in_specs = (
        P(None, ("groups", "ctx"), "chan"),
        P(None, None, "chan"),
        P(None, "chan"),
        P(None, "chan"),
        P("chan"),
        P("chan", None),
    )
    out_specs = P(("groups", "ctx"), "chan")
    return jax.shard_map(body, mesh=mesh, in_specs=in_specs, out_specs=out_specs, check_vma=False)
```
